256 devices in a mesh: dp: 32 (over y, z_lo, core), tensor: 8 (over z_hi, x).
Axes of the slice: x: 4, y: 4, z: 8 (z_hi: 2, z_lo: 4; z = z_hi * 4 + z_lo), core: 2. Of those that a mesh axis runs over, the one named last changes fastest.
Arguments:
- momentum: float32 [32, 4, 128, 8192], P('dp', None, None, 'tensor'), may hold values from -200 to 200
- gradient: bfloat16 [32, 4, 128, 8192], P('dp', None, None, 'tensor'), may hold values from -2 to 2
- kept_index: int32 [32, 4, 2, 128, 32], P(None, None, None, 'tensor'), may hold values from 0 to 4095, as said below
Outputs:
- momentum_out: float32 [32, 4, 128, 8192], P('dp', None, None, 'tensor')
- update: float32 [4, 128, 8192], P(None, None, 'tensor')
The draws below stay inside these ranges and needn't reach their ends.
Inputs may be any that keep to these rules, and one draw needn't show every extreme that they name: `kept_index`: for each replica and block the 32 positions are distinct, each f_r * 64 + f_c with f_r, f_c below 64.
All inputs are finite; a program needn't handle non-finite values.
Results may differ from the reference program's by a relative error of at most 0.0003.
Values sent between devices are 32-bit elements; how exact they have to be, the bound alone decides.
No kernel may reach another device: no remote copies, remote signals or barrier semaphores. Data moves between devices by JAX's collectives and lax.ppermute only.
A program may use at most 64 MiB of HBM per device.

```python
import math
import jax
import jax.numpy as jnp
from jax import lax

D = 8192
LAYERS = 4
ROWS = 128
GROUP = 64
TOPK = 32
REPLICAS = 32


def draw_momentum(key, part):
    key = jax.random.fold_in(key, 11)
    second = jax.random.fold_in(key, 1)
    third = jax.random.fold_in(key, 2)
    fourth = jax.random.fold_in(key, 3)
    shape = (REPLICAS, LAYERS, ROWS, D)
    columns = jnp.arange(D, dtype=jnp.float32) / D
    base = jnp.clip(jax.random.normal(second, shape, jnp.float32), -4.0, 4.0)
    rising = jnp.exp(math.log(3.0) * columns)
    row_scale = jnp.exp(jax.random.uniform(third, (1, LAYERS, ROWS, 1), jnp.float32, 0.0, math.log(10.0)))
    rough = jnp.exp(jax.random.uniform(fourth, (1, LAYERS, 1, D), jnp.float32, 0.0, math.log(3.3)))
    return (0.1 * base * row_scale * rising * rough).astype(jnp.float32)


def draw_kept_index(key, part):
    key = jax.random.fold_in(key, 23)
    cells = GROUP * GROUP
    freqs = jnp.arange(cells, dtype=jnp.int32)
    penalty = (freqs // GROUP + freqs % GROUP) * 256
    blocks_each = LAYERS * (ROWS // GROUP) * (D // GROUP)

    def one_replica(replica_key):
        scores = jax.random.randint(replica_key, (blocks_each, cells), 0, 2 ** 18, dtype=jnp.int32) - penalty
        scores = scores * cells + freqs
        chosen = lax.top_k(scores, TOPK)[1]
        return chosen.astype(jnp.int32)
    keys = jax.random.split(key, REPLICAS)
    picked = lax.map(one_replica, keys)
    return picked.reshape(REPLICAS, LAYERS, ROWS // GROUP, D // GROUP, TOPK)


def block_levels(rng, dims, pieces, smallest, top_value):
    loudness = 1.0
    for dim, shards_of in pieces:
        heights = jax.random.uniform(jax.random.fold_in(jax.random.fold_in(rng, 6), dim), (shards_of,), jnp.float32, smallest / len(pieces), top_value / len(pieces))
        loudness = loudness * jnp.repeat(jnp.exp(heights), dims[dim] // shards_of).reshape((-1,) + (1,) * (len(dims) - 1 - dim))
    return loudness


def gaussian(rng, extent, scale, reach, pieces=(), held_as=jnp.bfloat16):
    factor_of = block_levels(rng, extent, pieces, -0.22, 0.18) if pieces else 1.0
    drawn = jax.random.normal(rng, extent, jnp.float32) * scale * factor_of
    return jnp.minimum(jnp.maximum(drawn, -reach), reach).astype(held_as)


def setup_inputs(seed: int = 0) -> dict:
    key_list = jax.random.split(jax.random.key(seed), 4)
    momentum = draw_momentum(jax.random.fold_in(key_list[3], 71), 0)
    gradient = gaussian(key_list[1], (REPLICAS, LAYERS, ROWS, D), 0.3, 2.0, ((0, 32), (3, 8)))
    kept_index = draw_kept_index(jax.random.fold_in(key_list[3], 71), 0)
    return {"momentum": momentum, "gradient": gradient, "kept_index": kept_index}


decay_rate = 0.999
epsilon = 1e-06

def cosine_rows(frequency, length):
    points = jnp.arange(length, dtype=jnp.float32)
    waves = frequency.astype(jnp.float32)[..., None]
    factor = jnp.where(frequency == 0, math.sqrt(1.0 / length), math.sqrt(2.0 / length))[..., None]
    return factor * jnp.cos(math.pi * (2.0 * points + 1.0) * waves / (2.0 * length))

def reference(momentum, gradient, kept_index):
    whole_basis = cosine_rows(jnp.arange(GROUP, dtype=jnp.int32), GROUP)
    layers, rows, cols = (momentum.shape[1], momentum.shape[2], momentum.shape[3])
    group_count = layers * (rows // GROUP) * (cols // GROUP)
    row_ids = jnp.arange(group_count, dtype=jnp.int32)[:, None]

    def spectrum_of(accumulated):
        blocks = accumulated.reshape(layers, rows // GROUP, GROUP, cols // GROUP, GROUP)
        spectrum = jnp.einsum('kr,larcb,mb->lackm', whole_basis, blocks, whole_basis, precision=lax.Precision.HIGHEST)
        return spectrum.reshape(group_count, GROUP * GROUP)

    def decode(coef_grid):
        shaped = coef_grid.reshape(layers, rows // GROUP, cols // GROUP, GROUP, GROUP)
        blocks = jnp.einsum('kr,lackm,mb->larcb', whole_basis, shaped, whole_basis, precision=lax.Precision.HIGHEST)
        return blocks.reshape(layers, rows, cols)

    def one_replica(running, trio):
        accumulated = decay_rate * trio[0] + trio[1].astype(jnp.float32)
        spectrum = spectrum_of(accumulated)
        positions = trio[2].reshape(group_count, TOPK).astype(jnp.int32)
        own_values = jnp.take_along_axis(spectrum, positions, axis=1)
        own_grid = jnp.zeros_like(spectrum).at[row_ids, positions].add(own_values)
        return (running + own_grid, accumulated - decode(own_grid))
    start_grid = jnp.zeros((group_count, GROUP * GROUP), jnp.float32)
    summed, momentum_out = lax.scan(one_replica, start_grid, (momentum, gradient, kept_index))
    decoded = decode(summed)
    mean_square = lax.optimization_barrier(jnp.mean(decoded * decoded, axis=(1, 2)))
    update = decoded * lax.rsqrt(mean_square + epsilon)[:, None, None]
    return (momentum_out, update)
```

```python
import math

import jax
import jax.numpy as jnp
import ml_dtypes
import numpy as np
from jax import lax
from jax.experimental import pallas as pl
from jax.experimental.pallas import tpu as pltpu
from jax.sharding import PartitionSpec as P

GROUP = 64
TOPK = 32
REPLICAS = 32
LAYERS = 4
ROWS = 128
COLS = 1024
TILES = COLS // 256
BLOCKS = 128

decay_rate = 0.999
epsilon = 1e-06

BF = jnp.bfloat16
F32 = jnp.float32


def basis_matrix():
    f = np.arange(GROUP, dtype=np.float64)[:, None]
    n = np.arange(GROUP, dtype=np.float64)[None, :]
    scale = np.where(f == 0, math.sqrt(1.0 / GROUP), math.sqrt(2.0 / GROUP))
    return scale * np.cos(math.pi * (2.0 * n + 1.0) * f / (2.0 * GROUP))


def halves(x):
    x = x.astype(np.float32)
    hi = x.astype(ml_dtypes.bfloat16)
    lo = (x - hi.astype(np.float32)).astype(ml_dtypes.bfloat16)
    return hi, lo


def constants():
    b = basis_matrix()
    two, four = np.kron(np.eye(2), b), np.kron(np.eye(4), b)
    row_hi, row_lo = halves(two)
    col_hi, col_lo = halves(four)
    forward_rows = np.concatenate([row_hi, row_hi, row_lo], axis=1)
    forward_cols = np.concatenate([col_hi, col_lo], axis=0)
    back_hi, back_lo = halves(two.T)
    back_rows = np.concatenate([back_hi, back_hi, back_lo], axis=1)
    return forward_rows, forward_cols, back_rows


def split(x):
    hi = x.astype(BF)
    return hi, (x - hi.astype(F32)).astype(BF)


def mm(a, b):
    return jnp.dot(a, b, preferred_element_type=F32)


def mm_t(a, b):
    return lax.dot_general(a, b, (((1,), (1,)), ((), ())), preferred_element_type=F32)


def rows_apply(rows, x):
    hi, lo = split(x)
    return mm(rows[:, :256], jnp.concatenate([hi, lo], axis=0)) + mm(rows[:, 256:], hi)


def cols_apply(x, cols):
    hi, lo = split(x)
    both = mm(jnp.concatenate([hi, lo], axis=0), cols[:256])
    return both[:128] + both[128:] + mm(hi, cols[256:])


def own_rows(idx_ref):
    return jnp.concatenate([idx_ref[pl.ds(cj, 32, stride=4), :] for cj in range(4)], axis=1)


def lane_block(shape):
    return lax.shift_right_logical(lax.broadcasted_iota(jnp.int32, shape, len(shape) - 1), 5) & 3


def pick_kernel(p_ref, m_ref, g_ref, idx_ref, rows_ref, cols_ref, v_ref, own_ref):
    layer = pl.program_id(0)

    @pl.when(layer == 0)
    def _():
        own_ref[...] = own_rows(idx_ref)

    acc = decay_rate * m_ref[0] + g_ref[0].astype(F32)
    y = rows_apply(rows_ref[...], acc)
    y_hi, y_lo = split(y)
    freq = lax.broadcasted_iota(jnp.int32, (GROUP, 128), 0)
    place = lax.broadcasted_iota(jnp.int32, (256, 256), 0)
    zeros = jnp.zeros((GROUP, 128), BF)
    for t in range(TILES):
        s = slice(t * 256, t * 256 + 256)
        both = mm_t(cols_ref[:256], jnp.concatenate([y_hi[:, s], y_lo[:, s]], axis=0))
        spec = both[:, :128] + both[:, 128:] + mm_t(cols_ref[256:], y_hi[:, s])
        spec_hi, spec_lo = split(spec)
        pos = [own_ref[pl.ds(layer * 8 + a * 4 + t, 1), :] for a in range(2)]
        fr = [lax.shift_right_logical(x, 6) for x in pos]
        hot = [(freq == x).astype(F32).astype(BF) for x in fr]
        pick = jnp.concatenate(
            [
                jnp.concatenate([hot[0], zeros], axis=1),
                jnp.concatenate([zeros, hot[1]], axis=1),
            ],
            axis=0,
        )
        got = mm(jnp.concatenate([spec_hi, spec_lo], axis=1), jnp.concatenate([pick, pick], axis=0))
        where = jnp.concatenate([(x & 63) + 64 * lane_block((1, 128)) for x in pos], axis=1)
        v = jnp.sum(jnp.where(place == where, got, 0.0), axis=0, keepdims=True)
        for a in range(2):
            v_ref[pl.ds(layer * 8 + a * 4 + t, 1), :] = v[:, a * 128 : a * 128 + 128]


def own_kernel(m_ref, g_ref, own_ref, v_ref, rows_ref, cols_ref, out_ref):
    layer = pl.program_id(0)
    freq = lax.broadcasted_iota(jnp.int32, (GROUP, 128), 0)
    place = lax.broadcasted_iota(jnp.int32, (256, 128), 0)
    for t in range(TILES):
        s = slice(t * 256, t * 256 + 256)
        grids = []
        for a in range(2):
            row = layer * 8 + a * 4 + t
            pos = own_ref[pl.ds(row, 1), :]
            v = v_ref[pl.ds(row, 1), :]
            left = jnp.where(freq == lax.shift_right_logical(pos, 6), v, 0.0)
            hi, lo = split(left)
            right = (place == (pos & 63) + 64 * lane_block((1, 128))).astype(F32).astype(BF)
            both = mm_t(jnp.concatenate([hi, lo], axis=0), right)
            grids.append(both[:GROUP] + both[GROUP:])
        grid = jnp.concatenate(grids, axis=0)
        back = cols_apply(rows_apply(rows_ref[...], grid), cols_ref[...])
        out_ref[0, :, s] = decay_rate * m_ref[0, :, s] + g_ref[0, :, s].astype(F32) - back


def arrange_kernel(p_ref, idx_ref, fr_ref, fc_ref):
    p = p_ref[0]
    for q in range(REPLICAS // 4):
        pos = jnp.concatenate([idx_ref[pl.ds((p ^ (4 * q + j)) * BLOCKS, BLOCKS), :] for j in range(4)], axis=1)
        fr_ref[:, q * 128 : q * 128 + 128] = lax.shift_right_logical(pos, 6).astype(F32)
        fc_ref[:, q * 128 : q * 128 + 128] = (pos & 63).astype(F32)


def sum_kernel(v_ref, fr_ref, fc_ref, rows_ref, cols_ref, out_ref, sq_ref, val_ref, grid_ref):
    layer = pl.program_id(0)
    lane = lane_block((8, 128))

    for q in range(REPLICAS // 4):
        x = [v_ref[4 * q + j, pl.ds(layer * 8, 8), :] for j in range(4)]
        for cj in range(4):
            y = jnp.zeros((8, 128), F32)
            for j in range(4):
                moved = x[j] if j == cj else pltpu.roll(x[j], ((j - cj) * 32) % 128, 1)
                y = jnp.where(lane == j, moved, y)
            val_ref[cj, :, q * 128 : q * 128 + 128] = y

    freq = lax.broadcasted_iota(jnp.int32, (GROUP, 1024), 0).astype(F32).astype(BF)

    def body(i, carry):
        grids = []
        for cj in range(4):
            row = layer * 32 + i * 4 + cj
            fr = fr_ref[pl.ds(row, 1), :].astype(BF)
            fc = fc_ref[pl.ds(row, 1), :].astype(BF)
            hi, lo = split(val_ref[cj, pl.ds(i, 1), :])
            at = freq == fr
            zero = jnp.zeros((), BF)
            left = jnp.concatenate([jnp.where(at, hi, zero), jnp.where(at, lo, zero)], axis=0)
            right = jnp.where(freq == fc, jnp.ones((), BF), zero)
            both = mm_t(left, right)
            grids.append(both[:GROUP] + both[GROUP:])
        a, cq = i // 4, i % 4
        grid_ref[cq, pl.ds(pl.multiple_of(a * GROUP, GROUP), GROUP), :] = jnp.concatenate(grids, axis=1)
        return carry

    lax.fori_loop(0, 8, body, 0)
    squares = jnp.zeros((1, 256), F32)
    for t in range(TILES):
        s = slice(t * 256, t * 256 + 256)
        grid = grid_ref[t]
        squares = squares + jnp.sum(grid * grid, axis=0, keepdims=True)
        out_ref[0, :, s] = cols_apply(rows_apply(rows_ref[...], grid), cols_ref[...])
    sq_ref[0] = squares[:, :128] + squares[:, 128:]


def whole(shape):
    return pl.BlockSpec(shape, lambda *_: (0,) * len(shape))


def params():
    return pltpu.CompilerParams(vmem_limit_bytes=40 * 2**20)


def pick(p, m, g, idx, rows, cols):
    layer = lambda l, p: (l, 0, 0)
    return pl.pallas_call(
        pick_kernel,
        grid_spec=pltpu.PrefetchScalarGridSpec(
            num_scalar_prefetch=1,
            grid=(LAYERS,),
            in_specs=[
                pl.BlockSpec((1, ROWS, COLS), layer),
                pl.BlockSpec((1, ROWS, COLS), layer),
                pl.BlockSpec((BLOCKS, TOPK), lambda l, p: (p[0], 0)),
                whole(rows.shape),
                whole(cols.shape),
            ],
            out_specs=[whole((32, 128)), whole((32, 128))],
        ),
        out_shape=[jax.ShapeDtypeStruct((32, 128), F32), jax.ShapeDtypeStruct((32, 128), jnp.int32)],
        compiler_params=params(),
        name="pick",
    )(p, m, g, idx, rows, cols)


def own_update(m, g, own, v, rows, cols):
    layer = lambda l: (l, 0, 0)
    return pl.pallas_call(
        own_kernel,
        grid=(LAYERS,),
        in_specs=[
            pl.BlockSpec((1, ROWS, COLS), layer),
            pl.BlockSpec((1, ROWS, COLS), layer),
            whole((32, 128)),
            whole((32, 128)),
            whole(rows.shape),
            whole(cols.shape),
        ],
        out_specs=pl.BlockSpec((1, ROWS, COLS), layer),
        out_shape=jax.ShapeDtypeStruct((LAYERS, ROWS, COLS), F32),
        compiler_params=params(),
        name="own",
    )(m, g, own, v, rows, cols)


def arrange(p, idx):
    return pl.pallas_call(
        arrange_kernel,
        grid_spec=pltpu.PrefetchScalarGridSpec(
            num_scalar_prefetch=1,
            grid=(1,),
            in_specs=[whole(idx.shape)],
            out_specs=[whole((BLOCKS, 1024)), whole((BLOCKS, 1024))],
        ),
        out_shape=[jax.ShapeDtypeStruct((BLOCKS, 1024), F32)] * 2,
        compiler_params=params(),
        name="arrange",
    )(p, idx)


def sum_decode(v, fr, fc, rows, cols):
    layer = lambda l: (l, 0, 0)
    return pl.pallas_call(
        sum_kernel,
        grid=(LAYERS,),
        in_specs=[
            whole(v.shape),
            whole(fr.shape),
            whole(fc.shape),
            whole(rows.shape),
            whole(cols.shape),
        ],
        out_specs=[pl.BlockSpec((1, ROWS, COLS), layer), pl.BlockSpec((1, 1, 128), layer)],
        out_shape=[
            jax.ShapeDtypeStruct((LAYERS, ROWS, COLS), F32),
            jax.ShapeDtypeStruct((LAYERS, 1, 128), F32),
        ],
        scratch_shapes=[pltpu.VMEM((4, 8, 1024), F32), pltpu.VMEM((TILES, 128, 256), F32)],
        compiler_params=params(),
        name="sum_decode",
    )(v, fr, fc, rows, cols)


def gather_values(v):
    def turn(x, bit):
        return lax.ppermute(x, "dp", [(i, i ^ bit) for i in range(REPLICAS)])

    v = v[None, None]
    v = jnp.concatenate([v] + [turn(v, b) for b in (2, 4, 6)], axis=0)
    v = jnp.concatenate([v] + [turn(v, b) for b in (8, 16, 24)], axis=0)
    v = jnp.concatenate([v, turn(v, 1)], axis=1)
    return v.reshape(REPLICAS, 32, 128)


def on_device(momentum, gradient, kept_index):
    m, g = momentum[0], gradient[0]
    idx = kept_index.reshape(REPLICAS * BLOCKS, TOPK)
    forward_rows, forward_cols, back_rows = (jnp.asarray(x) for x in constants())
    p = lax.axis_index("dp").astype(jnp.int32).reshape(1)
    v, own = pick(p, m, g, idx, forward_rows, forward_cols)
    values = gather_values(v)
    fr, fc = arrange(p, idx)
    momentum_out = own_update(m, g, own, v, back_rows, forward_cols)
    decoded, squares = sum_decode(values, fr, fc, back_rows, forward_cols)
    squares = jnp.sum(squares, axis=(1, 2))
    total = squares
    for bits in ((1, 2, 3), (4,)):
        total = total + sum(
            lax.ppermute(total, "tensor", [(i, i ^ b) for i in range(8)]) for b in bits
        )
    entries = ROWS * COLS * lax.axis_size("tensor")
    update = decoded * lax.rsqrt(total / entries + epsilon)[:, None, None]
    return (momentum_out[None], update)


def solution(mesh):
    placed = (
        P("dp", None, None, "tensor"),
        P("dp", None, None, "tensor"),
        P(None, None, None, "tensor", None),
    )
    return jax.shard_map(
        on_device,
        mesh=mesh,
        in_specs=placed,
        out_specs=(P("dp", None, None, "tensor"), P(None, None, "tensor")),
        check_vma=False,
    )
```

```python
import math

import jax
import jax.numpy as jnp
import ml_dtypes
import numpy as np
from jax import lax
from jax.experimental import pallas as pl
from jax.experimental.pallas import tpu as pltpu
from jax.sharding import PartitionSpec as P

GROUP = 64
TOPK = 32
REPLICAS = 32
LAYERS = 4
ROWS = 128
COLS = 1024
TILES = COLS // 256
BLOCKS = 128
SET = 8
ENTRIES = 128 * 8192

decay_rate = 0.999
epsilon = 1e-06

BF = jnp.bfloat16
F32 = jnp.float32


def basis_matrix():
    f = np.arange(GROUP, dtype=np.float64)[:, None]
    n = np.arange(GROUP, dtype=np.float64)[None, :]
    scale = np.where(f == 0, math.sqrt(1.0 / GROUP), math.sqrt(2.0 / GROUP))
    return scale * np.cos(math.pi * (2.0 * n + 1.0) * f / (2.0 * GROUP))


def halves(x):
    x = x.astype(np.float32)
    hi = x.astype(ml_dtypes.bfloat16)
    lo = (x - hi.astype(np.float32)).astype(ml_dtypes.bfloat16)
    return hi, lo


def constants():
    b = basis_matrix()
    two, four = np.kron(np.eye(2), b), np.kron(np.eye(4), b)
    t_hi, t_lo = halves(two.T)
    none = np.zeros_like(t_lo)
    forward_cols = np.concatenate(halves(four.T), axis=0)
    forward_rows = np.block([[t_hi, t_lo], [t_hi, none]])
    back_cols = np.concatenate(halves(four), axis=0)
    back_rows = np.block([[t_hi, t_hi], [t_lo, none]])
    return forward_cols, forward_rows, back_cols, back_rows


def split(x):
    hi = x.astype(BF)
    return hi, (x - hi.astype(F32)).astype(BF)


def mm(a, b):
    return jnp.dot(a, b, preferred_element_type=F32)


def mm_t(a, b):
    return lax.dot_general(a, b, (((1,), (1,)), ((), ())), preferred_element_type=F32)


def cols_apply(x, cols):
    n = x.shape[0]
    hi, lo = split(x)
    both = mm(jnp.concatenate([hi, lo], axis=0), cols[:256])
    return both[:n] + both[n:] + mm(hi, cols[256:])


def back(grids, cols, rows):
    half = cols_apply(jnp.concatenate(grids, axis=0), cols)
    out = []
    for t in range(TILES):
        hi, lo = split(half[t * 128 : t * 128 + 128])
        both = mm(rows, jnp.concatenate([hi, lo], axis=0))
        out.append(both[:128] + both[128:])
    return out


def lane_block(shape):
    return lax.shift_right_logical(lax.broadcasted_iota(jnp.int32, shape, len(shape) - 1), 5) & 3


def pick_kernel(m_hbm, g_hbm, idx_hbm, cols_hbm, rows_hbm, v_ref, own_ref, m_buf, g_buf, idx_buf, cols_ref, rows_ref, sems):
    p = lax.axis_index("dp")
    copies = [pltpu.make_async_copy(idx_hbm.at[pl.ds(p * BLOCKS, BLOCKS)], idx_buf, sems.at[0])]
    copies += [pltpu.make_async_copy(cols_hbm, cols_ref, sems.at[1])]
    copies += [pltpu.make_async_copy(rows_hbm, rows_ref, sems.at[2])]
    for l in range(LAYERS):
        copies.append(pltpu.make_async_copy(m_hbm.at[l], m_buf.at[l], sems.at[3 + 2 * l]))
        copies.append(pltpu.make_async_copy(g_hbm.at[l], g_buf.at[l], sems.at[4 + 2 * l]))
    order = [3, 4, 1, 0, 2] + list(range(5, 3 + 2 * LAYERS))
    for i in order:
        copies[i].start()
    for i in range(3):
        copies[i].wait()
    own_ref[...] = jnp.concatenate([idx_buf[pl.ds(cj, 32, stride=4), :] for cj in range(4)], axis=1)
    freq = lax.broadcasted_iota(jnp.int32, (GROUP, 128), 0)
    place = lax.broadcasted_iota(jnp.int32, (256, 256), 0)
    zeros = jnp.zeros((GROUP, 128), BF)
    for l in range(LAYERS):
        copies[3 + 2 * l].wait()
        copies[4 + 2 * l].wait()
        acc = decay_rate * m_buf[l] + g_buf[l].astype(F32)
        tiles = jnp.concatenate([acc[:, t * 256 : t * 256 + 256] for t in range(TILES)], axis=0)
        half = cols_apply(tiles, cols_ref)
        for t in range(TILES):
            hi, lo = split(half[t * 128 : t * 128 + 128].T)
            both = mm(jnp.concatenate([hi, lo], axis=1), rows_ref[...])
            hi, lo = split(both[:, :128] + both[:, 128:])
            pos = [own_ref[pl.ds(l * 8 + a * 4 + t, 1), :] for a in range(2)]
            hot = [(freq == lax.shift_right_logical(x, 6)).astype(F32).astype(BF) for x in pos]
            pick = jnp.concatenate(
                [
                    jnp.concatenate([hot[0], zeros], axis=1),
                    jnp.concatenate([zeros, hot[1]], axis=1),
                ],
                axis=0,
            )
            got = mm(jnp.concatenate([hi, lo], axis=1), jnp.concatenate([pick, pick], axis=0))
            where = jnp.concatenate([(x & 63) + 64 * lane_block((1, 128)) for x in pos], axis=1)
            v = jnp.sum(jnp.where(place == where, got, 0.0), axis=0, keepdims=True)
            for a in range(2):
                v_ref[pl.ds(l * 8 + a * 4 + t, 1), :] = v[:, a * 128 : a * 128 + 128]


def own_kernel(m_ref, g_ref, own_ref, v_ref, cols_ref, rows_ref, out_hbm, out_buf, sems):
    freq = lax.broadcasted_iota(jnp.int32, (GROUP, 128), 0)
    place = lax.broadcasted_iota(jnp.int32, (256, 128), 0)
    copies = []
    for l in range(LAYERS):
        grids = []
        for t in range(TILES):
            parts = []
            for a in range(2):
                row = l * 8 + a * 4 + t
                pos = own_ref[pl.ds(row, 1), :]
                v = v_ref[pl.ds(row, 1), :]
                hi, lo = split(jnp.where(freq == lax.shift_right_logical(pos, 6), v, 0.0))
                right = (place == (pos & 63) + 64 * lane_block((1, 128))).astype(F32).astype(BF)
                both = mm_t(jnp.concatenate([hi, lo], axis=0), right)
                parts.append(both[:GROUP] + both[GROUP:])
            grids.append(jnp.concatenate(parts, axis=0))
        for t, tile in enumerate(back(grids, cols_ref, rows_ref[...])):
            s = slice(t * 256, t * 256 + 256)
            acc = decay_rate * m_ref[l, :, s] + g_ref[l, :, s].astype(F32)
            out_buf[l, :, s] = acc - tile
        copies.append(pltpu.make_async_copy(out_buf.at[l], out_hbm.at[l], sems.at[l]))
        copies[-1].start()
    for copy in copies:
        copy.wait()


def arrange_kernel(idx_ref, fr_ref, fc_ref):
    p = lax.axis_index("dp")
    for q in range(REPLICAS // 4):
        pos = jnp.concatenate([idx_ref[pl.ds((p ^ (4 * q + j)) * BLOCKS, BLOCKS), :] for j in range(4)], axis=1)
        fr_ref[:, q * 128 : q * 128 + 128] = lax.shift_right_logical(pos, 6).astype(F32)
        fc_ref[:, q * 128 : q * 128 + 128] = (pos & 63).astype(F32)


def set_kernel(number, first, last, v_ref, fr_ref, fc_ref, *rest):
    old_ref = None
    if not first:
        old_ref, rest = rest[0], rest[1:]
    if last:
        grid_ref, sq_ref, val_ref = rest
        sq_ref[...] = jnp.zeros_like(sq_ref)
    else:
        grid_ref, val_ref = rest
    lane = lane_block((32, 128))
    for q in range(SET // 4):
        x = [v_ref[4 * q + j] for j in range(4)]
        for cj in range(4):
            y = jnp.zeros((32, 128), F32)
            for j in range(4):
                moved = x[j] if j == cj else pltpu.roll(x[j], ((j - cj) * 32) % 128, 1)
                y = jnp.where(lane == j, moved, y)
            val_ref[cj, :, q * 128 : q * 128 + 128] = y
    wide = 32 * SET
    freq = lax.broadcasted_iota(jnp.int32, (GROUP, wide), 0).astype(F32).astype(BF)
    s = slice(number * wide, number * wide + wide)
    zero, one = jnp.zeros((), BF), jnp.ones((), BF)

    def body(l, carry):
        squares = jnp.zeros((1, 256), F32)
        for i in range(2 * TILES):
            a, t = i // TILES, i % TILES
            parts = []
            for cj in range(4):
                row = l * 32 + i * 4 + cj
                fr = fr_ref[pl.ds(row, 1), s].astype(BF)
                fc = fc_ref[pl.ds(row, 1), s].astype(BF)
                hi, lo = split(val_ref[cj, pl.ds(l * 8 + i, 1), :])
                at = freq == fr
                left = jnp.concatenate([jnp.where(at, hi, zero), jnp.where(at, lo, zero)], axis=0)
                both = mm_t(left, jnp.where(freq == fc, one, zero))
                parts.append(both[:GROUP] + both[GROUP:])
            grid = jnp.concatenate(parts, axis=1)
            if old_ref is not None:
                grid = grid + old_ref[l, t, a * GROUP : a * GROUP + GROUP, :]
            grid_ref[l, t, a * GROUP : a * GROUP + GROUP, :] = grid
            if last:
                squares = squares + jnp.sum(grid * grid, axis=0, keepdims=True)
        if last:
            sq_ref[pl.ds(l, 1), :] = squares[:, :128] + squares[:, 128:]
        return carry

    lax.fori_loop(0, LAYERS, body, 0)


def decode_kernel(grid_ref, cols_ref, rows_ref, out_ref):
    def body(l, carry):
        tiles = back([grid_ref[l, t] for t in range(TILES)], cols_ref, rows_ref[...])
        for t, tile in enumerate(tiles):
            out_ref[l, :, t * 256 : t * 256 + 256] = tile
        return carry

    lax.fori_loop(0, LAYERS, body, 0)


def scale_kernel(x_ref, a_ref, b_ref, out_hbm, out_buf, sems):
    total = jnp.sum(a_ref[...] + b_ref[...], axis=1, keepdims=True)
    factor = lax.rsqrt(jnp.broadcast_to(total, (8, 128)) / ENTRIES + epsilon)
    copies = []
    for l in range(LAYERS):
        row = factor[l : l + 1]
        for t in range(COLS // 128):
            s = slice(t * 128, t * 128 + 128)
            out_buf[l, :, s] = x_ref[l, :, s] * row
        copies.append(pltpu.make_async_copy(out_buf.at[l], out_hbm.at[l], sems.at[l]))
        copies[-1].start()
    for copy in copies:
        copy.wait()


VM = pl.BlockSpec(memory_space=pltpu.VMEM)
HB = pl.BlockSpec(memory_space=pltpu.HBM)
DECODED = jax.ShapeDtypeStruct((LAYERS, ROWS, COLS), F32)
GRIDS = jax.ShapeDtypeStruct((LAYERS, TILES, 128, 256), F32)


def call(kernel, name, ins, outs, shapes, scratch=(), us=1.0, mib=32, **more):
    return pl.pallas_call(
        kernel,
        in_specs=ins,
        out_specs=outs,
        out_shape=shapes,
        scratch_shapes=list(scratch),
        compiler_params=pltpu.CompilerParams(vmem_limit_bytes=mib * 2**20),
        cost_estimate=pl.CostEstimate(flops=int(us * 1e9), bytes_accessed=int(us * 2e6), transcendentals=0),
        name=name,
        **more,
    )


def pick(m, g, idx, cols, rows):
    return call(
        pick_kernel,
        "pick",
        [HB] * 5,
        [VM] * 2,
        [jax.ShapeDtypeStruct((32, 128), F32), jax.ShapeDtypeStruct((32, 128), jnp.int32)],
        [
            pltpu.VMEM((LAYERS, ROWS, COLS), F32),
            pltpu.VMEM((LAYERS, ROWS, COLS), BF),
            pltpu.VMEM((BLOCKS, TOPK), jnp.int32),
            pltpu.VMEM(cols.shape, BF),
            pltpu.VMEM(rows.shape, BF),
            pltpu.SemaphoreType.DMA((3 + 2 * LAYERS,)),
        ],
        4.0,
        60,
    )(m, g, idx, cols, rows)


def own_update(m, g, own, v, cols, rows):
    return call(
        own_kernel,
        "own",
        [VM] * 6,
        HB,
        DECODED,
        [pltpu.VMEM((LAYERS, ROWS, COLS), F32), pltpu.SemaphoreType.DMA((LAYERS,))],
        3.0,
    )(m, g, own, v, cols, rows)


def arrange(idx):
    shape = jax.ShapeDtypeStruct((BLOCKS, 1024), F32)
    return call(arrange_kernel, "arrange", [VM], [VM, VM], [shape, shape], (), 0.5)(idx)


def add_set(number, last, v, fr, fc, old):
    ins, outs, shapes, more = [v, fr, fc], [VM], [GRIDS], {}
    first = old is None
    if not first:
        ins.append(old)
        more = dict(input_output_aliases={3: 0})
    if last:
        outs.append(VM)
        shapes.append(jax.ShapeDtypeStruct((8, 128), F32))
    return call(
        lambda *refs: set_kernel(number, first, last, *refs),
        f"set{number}",
        [VM] * len(ins),
        outs,
        shapes,
        [pltpu.VMEM((4, 32, 32 * SET), F32)],
        2.6,
        **more,
    )(*ins)


def decode(grid, cols, rows):
    return call(decode_kernel, "decode", [VM] * 3, VM, DECODED, (), 3.0)(grid, cols, rows)


def rescale(x, a, b):
    return call(
        scale_kernel,
        "rescale",
        [VM] * 3,
        HB,
        DECODED,
        [pltpu.VMEM((LAYERS, ROWS, COLS), F32), pltpu.SemaphoreType.DMA((LAYERS,))],
        1.0,
    )(x, a, b)


def turn(x, axis, size, bit):
    return lax.ppermute(x, axis, [(i, i ^ bit) for i in range(size)])


def on_device(momentum, gradient, kept_index):
    m, g = momentum[0], gradient[0]
    idx = kept_index.reshape(REPLICAS * BLOCKS, TOPK)
    forward_cols, forward_rows, back_cols, back_rows = (jnp.asarray(x) for x in constants())
    v, own = pick(m, g, idx, forward_cols, forward_rows)

    x = jnp.stack([v, turn(v, "dp", REPLICAS, 1)])
    x = jnp.concatenate([x] + [turn(x, "dp", REPLICAS, b) for b in (2, 4, 6)], axis=0)
    order = (0, 1, 3, 2)
    sets = {s: x if s == 0 else turn(x, "dp", REPLICAS, 8 * s) for s in order}
    fr, fc = arrange(idx)
    momentum_out = own_update(m, g, own, v, back_cols, back_rows)
    grid = None
    for s in order[:-1]:
        (grid,) = add_set(s, False, sets[s], fr, fc, grid)
    grid, squares = add_set(order[-1], True, sets[order[-1]], fr, fc, grid)

    total = squares
    for b in (1, 3):
        total = total + turn(total, "tensor", 8, b)
    other = turn(total, "tensor", 8, 4)
    decoded = decode(grid, back_cols, back_rows)
    update = rescale(decoded, total, other)
    return (momentum_out[None], update)


def solution(mesh):
    placed = (
        P("dp", None, None, "tensor"),
        P("dp", None, None, "tensor"),
        P(None, None, None, "tensor", None),
    )
    return jax.shard_map(
        on_device,
        mesh=mesh,
        in_specs=placed,
        out_specs=(P("dp", None, None, "tensor"), P(None, None, "tensor")),
        check_vma=False,
    )
```

```python
import math

import jax
import jax.numpy as jnp
import ml_dtypes
import numpy as np
from jax import lax
from jax.experimental import pallas as pl
from jax.experimental.pallas import tpu as pltpu
from jax.sharding import PartitionSpec as P

GROUP = 64
TOPK = 32
REPLICAS = 32
LAYERS = 4
ROWS = 128
COLS = 1024
TILES = COLS // 256
BLOCKS = 128
SET = 8
ENTRIES = 128 * 8192
HALF = LAYERS // 2

decay_rate = 0.999
epsilon = 1e-06

BF = jnp.bfloat16
F32 = jnp.float32


def basis_matrix():
    f = np.arange(GROUP, dtype=np.float64)[:, None]
    n = np.arange(GROUP, dtype=np.float64)[None, :]
    scale = np.where(f == 0, math.sqrt(1.0 / GROUP), math.sqrt(2.0 / GROUP))
    return scale * np.cos(math.pi * (2.0 * n + 1.0) * f / (2.0 * GROUP))


def halves(x):
    x = x.astype(np.float32)
    hi = x.astype(ml_dtypes.bfloat16)
    lo = (x - hi.astype(np.float32)).astype(ml_dtypes.bfloat16)
    return hi, lo


def constants():
    b = basis_matrix()
    two, four = np.kron(np.eye(2), b), np.kron(np.eye(4), b)
    t_hi, t_lo = halves(two.T)
    none = np.zeros_like(t_lo)
    forward_cols = np.concatenate(halves(four.T), axis=0)
    forward_rows = np.block([[t_hi, t_lo], [t_hi, none]])
    back_cols = np.concatenate(halves(four), axis=0)
    back_rows = np.block([[t_hi, t_hi], [t_lo, none]])
    return forward_cols, forward_rows, back_cols, back_rows


def split(x):
    hi = x.astype(BF)
    return hi, (x - hi.astype(F32)).astype(BF)


def mm(a, b):
    return jnp.dot(a, b, preferred_element_type=F32)


def mm_t(a, b):
    return lax.dot_general(a, b, (((1,), (1,)), ((), ())), preferred_element_type=F32)


def cols_apply(x, cols):
    n = x.shape[0]
    hi, lo = split(x)
    both = mm(jnp.concatenate([hi, lo], axis=0), cols[:256])
    return both[:n] + both[n:] + mm(hi, cols[256:])


def back(grids, cols, rows):
    half = cols_apply(jnp.concatenate(grids, axis=0), cols)
    out = []
    for t in range(TILES):
        hi, lo = split(half[t * 128 : t * 128 + 128])
        both = mm(rows, jnp.concatenate([hi, lo], axis=0))
        out.append(both[:128] + both[128:])
    return out


def lane_block(shape):
    return lax.shift_right_logical(lax.broadcasted_iota(jnp.int32, shape, len(shape) - 1), 5) & 3


def pick_kernel(m_hbm, g_hbm, idx_hbm, cols_hbm, rows_hbm, v_ref, own_ref, mine_ref, theirs_ref, acc_ref, m_buf, g_buf, idx_buf, cols_ref, rows_ref, sems):
    p = lax.axis_index("dp")
    core = p & 1
    small = [
        pltpu.make_async_copy(cols_hbm, cols_ref, sems.at[0]),
        pltpu.make_async_copy(rows_hbm, rows_ref, sems.at[1]),
        pltpu.make_async_copy(idx_hbm.at[pl.ds(p * BLOCKS, BLOCKS)], idx_buf, sems.at[2]),
    ]
    large = [
        (
            pltpu.make_async_copy(m_hbm.at[l], m_buf.at[l], sems.at[3 + 2 * l]),
            pltpu.make_async_copy(g_hbm.at[l], g_buf.at[l], sems.at[4 + 2 * l]),
        )
        for l in range(LAYERS)
    ]
    for copy in (*large[0], *small, *large[1], *large[2], *large[3]):
        copy.start()
    freq = lax.broadcasted_iota(jnp.int32, (GROUP, 128), 0)
    place = lax.broadcasted_iota(jnp.int32, (256, 256), 0)
    zeros = jnp.zeros((GROUP, 128), BF)

    def columns(l):
        acc = decay_rate * m_buf[l] + g_buf[l].astype(F32)
        acc_ref[l] = acc
        tiles = jnp.concatenate([acc[:, t * 256 : t * 256 + 256] for t in range(TILES)], axis=0)
        return cols_apply(tiles, cols_ref)

    def rows_and_pick(l, half):
        for t in range(TILES):
            hi, lo = split(half[t * 128 : t * 128 + 128].T)
            both = mm(jnp.concatenate([hi, lo], axis=1), rows_ref[...])
            hi, lo = split(both[:, :128] + both[:, 128:])
            pos = [own_ref[pl.ds(l * 8 + a * 4 + t, 1), :] for a in range(2)]
            hot = [(freq == lax.shift_right_logical(x, 6)).astype(F32).astype(BF) for x in pos]
            pick = jnp.concatenate(
                [
                    jnp.concatenate([hot[0], zeros], axis=1),
                    jnp.concatenate([zeros, hot[1]], axis=1),
                ],
                axis=0,
            )
            got = mm(jnp.concatenate([hi, lo], axis=1), jnp.concatenate([pick, pick], axis=0))
            where = jnp.concatenate([(x & 63) + 64 * lane_block((1, 128)) for x in pos], axis=1)
            v = jnp.sum(jnp.where(place == where, got, 0.0), axis=0, keepdims=True)
            for a in range(2):
                v_ref[pl.ds(l * 8 + a * 4 + t, 1), :] = v[:, a * 128 : a * 128 + 128]

    before = None
    for l in range(LAYERS):
        for copy in large[l]:
            copy.wait()
        if l == 0:
            small[0].wait()
        if l == 1:
            small[1].wait()
            small[2].wait()
            own_ref[...] = jnp.concatenate([idx_buf[pl.ds(cj, 32, stride=4), :] for cj in range(4)], axis=1)
        half = columns(l)
        if before is not None:
            rows_and_pick(l - 1, before)
        before = half
    rows_and_pick(LAYERS - 1, before)
    mine_ref[...] = v_ref[pl.ds(pl.multiple_of(core * 16, 16), 16), :]
    theirs_ref[...] = v_ref[pl.ds(pl.multiple_of(16 - core * 16, 16), 16), :]


def own_kernel(layers, acc_ref, own_ref, v_ref, cols_ref, rows_ref, *rest):
    out_hbm, out_buf, sems = rest[-3:]
    freq = lax.broadcasted_iota(jnp.int32, (GROUP, 128), 0)
    place = lax.broadcasted_iota(jnp.int32, (256, 128), 0)
    copies = []
    for i, l in enumerate(layers):
        grids = []
        for t in range(TILES):
            parts = []
            for a in range(2):
                row = l * 8 + a * 4 + t
                pos = own_ref[pl.ds(row, 1), :]
                v = v_ref[pl.ds(row, 1), :]
                hi, lo = split(jnp.where(freq == lax.shift_right_logical(pos, 6), v, 0.0))
                right = (place == (pos & 63) + 64 * lane_block((1, 128))).astype(F32).astype(BF)
                both = mm_t(jnp.concatenate([hi, lo], axis=0), right)
                parts.append(both[:GROUP] + both[GROUP:])
            grids.append(jnp.concatenate(parts, axis=0))
        for t, tile in enumerate(back(grids, cols_ref, rows_ref[...])):
            s = slice(t * 256, t * 256 + 256)
            out_buf[i, :, s] = acc_ref[l, :, s] - tile
        copies.append(pltpu.make_async_copy(out_buf.at[i], out_hbm.at[l], sems.at[i]))
        copies[-1].start()
    for copy in copies:
        copy.wait()


def arrange_kernel(idx_ref, fr_ref, fc_ref):
    p = lax.axis_index("dp")
    half = BLOCKS // 2
    start = (p & 1) * half
    for q in range(REPLICAS // 4):
        pos = jnp.concatenate([idx_ref[pl.ds(pl.multiple_of((p ^ (4 * q + j)) * BLOCKS + start, half), half), :] for j in range(4)], axis=1)
        fr_ref[:, q * 128 : q * 128 + 128] = lax.shift_right_logical(pos, 6).astype(F32)
        fc_ref[:, q * 128 : q * 128 + 128] = (pos & 63).astype(F32)


def set_kernel(number, first, last, v_ref, fr_ref, fc_ref, *rest):
    old_ref = None
    if not first:
        old_ref, rest = rest[0], rest[1:]
    if last:
        grid_ref, sq_ref, val_ref = rest
        first_layer = (lax.axis_index("dp") & 1) * HALF
        sq_ref[...] = jnp.zeros_like(sq_ref)
    else:
        grid_ref, val_ref = rest
    lane = lane_block((16, 128))
    for q in range(SET // 4):
        x = [v_ref[4 * q + j] for j in range(4)]
        for cj in range(4):
            y = jnp.zeros((16, 128), F32)
            for j in range(4):
                moved = x[j] if j == cj else pltpu.roll(x[j], ((j - cj) * 32) % 128, 1)
                y = jnp.where(lane == j, moved, y)
            val_ref[cj, :, q * 128 : q * 128 + 128] = y
    wide = 32 * SET
    freq = lax.broadcasted_iota(jnp.int32, (GROUP, wide), 0).astype(F32).astype(BF)
    s = slice(number * wide, number * wide + wide)
    zero, one = jnp.zeros((), BF), jnp.ones((), BF)

    def body(l, carry):
        squares = jnp.zeros((1, 256), F32)
        for i in range(2 * TILES):
            a, t = i // TILES, i % TILES
            parts = []
            for cj in range(4):
                row = l * 32 + i * 4 + cj
                fr = fr_ref[pl.ds(row, 1), s].astype(BF)
                fc = fc_ref[pl.ds(row, 1), s].astype(BF)
                hi, lo = split(val_ref[cj, pl.ds(l * 8 + i, 1), :])
                at = freq == fr
                left = jnp.concatenate([jnp.where(at, hi, zero), jnp.where(at, lo, zero)], axis=0)
                both = mm_t(left, jnp.where(freq == fc, one, zero))
                parts.append(both[:GROUP] + both[GROUP:])
            grid = jnp.concatenate(parts, axis=1)
            if old_ref is not None:
                grid = grid + old_ref[l, t, a * GROUP : a * GROUP + GROUP, :]
            grid_ref[l, t, a * GROUP : a * GROUP + GROUP, :] = grid
            if last:
                squares = squares + jnp.sum(grid * grid, axis=0, keepdims=True)
        if last:
            sq_ref[pl.ds(first_layer + l, 1), :] = squares[:, :128] + squares[:, 128:]
        return carry

    for l in range(HALF):
        body(l, 0)


def decode_kernel(grid_ref, cols_ref, rows_ref, out_ref):
    def body(l, carry):
        tiles = back([grid_ref[l, t] for t in range(TILES)], cols_ref, rows_ref[...])
        for t, tile in enumerate(tiles):
            out_ref[l, :, t * 256 : t * 256 + 256] = tile
        return carry

    for l in range(HALF):
        body(l, 0)


def scale_kernel(mine_ref, theirs_ref, a_ref, b_ref, out_hbm, out_buf, factor_ref, sems):
    core = lax.axis_index("dp") & 1
    total = jnp.sum(a_ref[...] + b_ref[...], axis=1, keepdims=True)
    factor_ref[...] = lax.rsqrt(jnp.broadcast_to(total, (8, 128)) / ENTRIES + epsilon)
    copies = []
    for ref, start in ((mine_ref, core * HALF), (theirs_ref, HALF - core * HALF)):
        for i in range(HALF):
            l = start + i
            row = factor_ref[pl.ds(l, 1), :]
            for t in range(COLS // 128):
                s = slice(t * 128, t * 128 + 128)
                out_buf[l, :, s] = ref[i, :, s] * row
            copies.append(pltpu.make_async_copy(out_buf.at[l], out_hbm.at[l], sems.at[len(copies)]))
            copies[-1].start()
    for copy in copies:
        copy.wait()


VM = pl.BlockSpec(memory_space=pltpu.VMEM)
HB = pl.BlockSpec(memory_space=pltpu.HBM)
DECODED = jax.ShapeDtypeStruct((LAYERS, ROWS, COLS), F32)
GRIDS = jax.ShapeDtypeStruct((HALF, TILES, 128, 256), F32)
HALVED = jax.ShapeDtypeStruct((HALF, ROWS, COLS), F32)


def call(kernel, name, ins, outs, shapes, scratch=(), us=1.0, mib=32, **more):
    return pl.pallas_call(
        kernel,
        in_specs=ins,
        out_specs=outs,
        out_shape=shapes,
        scratch_shapes=list(scratch),
        compiler_params=pltpu.CompilerParams(vmem_limit_bytes=mib * 2**20),
        cost_estimate=pl.CostEstimate(flops=int(us * 1e9), bytes_accessed=int(us * 2e6), transcendentals=0),
        name=name,
        **more,
    )


def pick(m, g, idx, cols, rows):
    return call(
        pick_kernel,
        "pick",
        [HB] * 5,
        [VM] * 5,
        [
            jax.ShapeDtypeStruct((32, 128), F32),
            jax.ShapeDtypeStruct((32, 128), jnp.int32),
            jax.ShapeDtypeStruct((16, 128), F32),
            jax.ShapeDtypeStruct((16, 128), F32),
            DECODED,
        ],
        [
            pltpu.VMEM((LAYERS, ROWS, COLS), F32),
            pltpu.VMEM((LAYERS, ROWS, COLS), BF),
            pltpu.VMEM((BLOCKS, TOPK), jnp.int32),
            pltpu.VMEM(cols.shape, BF),
            pltpu.VMEM(rows.shape, BF),
            pltpu.SemaphoreType.DMA((3 + 2 * LAYERS,)),
        ],
        4.0,
    )(m, g, idx, cols, rows)


def own_update(layers, acc, own, v, cols, rows, out=None):
    ins, more = [acc, own, v, cols, rows], {}
    if out is not None:
        ins.append(out)
        more = dict(input_output_aliases={5: 0})
    return call(
        lambda *refs: own_kernel(layers, *refs),
        f"own{layers[0]}",
        [VM] * 5 + [HB] * (len(ins) - 5),
        HB,
        DECODED,
        [pltpu.VMEM((len(layers), ROWS, COLS), F32), pltpu.SemaphoreType.DMA((len(layers),))],
        2.2,
        **more,
    )(*ins)


def arrange(idx):
    shape = jax.ShapeDtypeStruct((BLOCKS // 2, 1024), F32)
    return call(arrange_kernel, "arrange", [VM], [VM, VM], [shape, shape], (), 0.5)(idx)


def add_set(number, last, v, fr, fc, old):
    ins, outs, shapes, more = [v, fr, fc], [VM], [GRIDS], {}
    first = old is None
    if not first:
        ins.append(old)
        more = dict(input_output_aliases={3: 0})
    if last:
        outs.append(VM)
        shapes.append(jax.ShapeDtypeStruct((8, 128), F32))
    return call(
        lambda *refs: set_kernel(number, first, last, *refs),
        f"set{number}",
        [VM] * len(ins),
        outs,
        shapes,
        [pltpu.VMEM((4, 16, 32 * SET), F32)],
        1.6,
        **more,
    )(*ins)


def decode(grid, cols, rows):
    return call(decode_kernel, "decode", [VM] * 3, VM, HALVED, (), 1.6)(grid, cols, rows)


def rescale(mine, theirs, a, b):
    return call(
        scale_kernel,
        "rescale",
        [VM] * 4,
        HB,
        DECODED,
        [pltpu.VMEM((LAYERS, ROWS, COLS), F32), pltpu.VMEM((8, 128), F32), pltpu.SemaphoreType.DMA((LAYERS,))],
        1.0,
    )(mine, theirs, a, b)


def turn(x, axis, size, bit):
    return lax.ppermute(x, axis, [(i, i ^ bit) for i in range(size)])


def near_other_core(x):
    pairs = [(p * 8 + t, (p ^ 1) * 8 + (t ^ 1)) for p in range(REPLICAS) for t in range(8)]
    return lax.ppermute(x, ("dp", "tensor"), pairs)


def across(x):
    pairs = []
    for y in range(4):
        for z in range(8):
            for core in range(2):
                for tx in range(4):
                    to = (z + 6) % 8 if z in (0, 1, 4, 5) else (z + 2) % 8
                    place = [((y * 4 + k % 4) * 2 + core) * 8 + (k // 4) * 4 + tx for k in (z, to)]
                    pairs.append(tuple(place))
    return lax.ppermute(x, ("dp", "tensor"), pairs)


def on_device(momentum, gradient, kept_index):
    m, g = momentum[0], gradient[0]
    idx = kept_index.reshape(REPLICAS * BLOCKS, TOPK)
    forward_cols, forward_rows, back_cols, back_rows = (jnp.asarray(x) for x in constants())
    held = [pltpu.with_memory_space_constraint(x, pltpu.HBM) for x in (m, g, idx, forward_cols, forward_rows)]
    v, own, mine, theirs, acc = pick(*held)

    x = jnp.stack([mine, turn(theirs, "dp", REPLICAS, 1)])
    x, v, idx = lax.optimization_barrier((x, v, idx))
    x = jnp.concatenate([x] + [turn(x, "dp", REPLICAS, b) for b in (2, 4, 6)], axis=0)
    fr, fc = arrange(idx)
    momentum_out = own_update((0, 1), acc, own, v, back_cols, back_rows)
    x, momentum_out = lax.optimization_barrier((x, momentum_out))
    order = (0, 1, 3, 2)
    sets = {s: x if s == 0 else turn(x, "dp", REPLICAS, 8 * s) for s in order}
    grid = None
    for s in order[:-1]:
        (grid,) = add_set(s, False, sets[s], fr, fc, grid)
    grid, squares = add_set(order[-1], True, sets[order[-1]], fr, fc, grid)

    other_grid = turn(grid, "dp", REPLICAS, 1)
    beside = turn(squares, "dp", REPLICAS, 1)
    near = turn(squares, "tensor", 8, 1)
    across_near = near_other_core(squares)
    squares, v = lax.optimization_barrier((squares, v))
    momentum_out = own_update((2, 3), acc, own, v, back_cols, back_rows, momentum_out)
    decoded = decode(grid, back_cols, back_rows)
    other = decode(other_grid, back_cols, back_rows)
    total = squares + beside + near + across_near
    total = total + turn(total, "tensor", 8, 3)
    update = rescale(decoded, other, total, across(total))
    return (momentum_out[None], update)


def solution(mesh):
    placed = (
        P("dp", None, None, "tensor"),
        P("dp", None, None, "tensor"),
        P(None, None, None, "tensor", None),
    )
    return jax.shard_map(
        on_device,
        mesh=mesh,
        in_specs=placed,
        out_specs=(P("dp", None, None, "tensor"), P(None, None, "tensor")),
        check_vma=False,
    )
```

```python
import math

import jax
import jax.numpy as jnp
import ml_dtypes
import numpy as np
from jax import lax
from jax.experimental import pallas as pl
from jax.experimental.pallas import tpu as pltpu
from jax.sharding import PartitionSpec as P

GROUP = 64
TOPK = 32
REPLICAS = 32
LAYERS = 4
ROWS = 128
COLS = 1024
TILES = COLS // 256
BLOCKS = 128
SET = 8
ENTRIES = 128 * 8192
HALF = LAYERS // 2

decay_rate = 0.999
epsilon = 1e-06

BF = jnp.bfloat16
F32 = jnp.float32


def basis_matrix():
    f = np.arange(GROUP, dtype=np.float64)[:, None]
    n = np.arange(GROUP, dtype=np.float64)[None, :]
    scale = np.where(f == 0, math.sqrt(1.0 / GROUP), math.sqrt(2.0 / GROUP))
    return scale * np.cos(math.pi * (2.0 * n + 1.0) * f / (2.0 * GROUP))


def halves(x):
    x = x.astype(np.float32)
    hi = x.astype(ml_dtypes.bfloat16)
    lo = (x - hi.astype(np.float32)).astype(ml_dtypes.bfloat16)
    return hi, lo


def constants():
    w_hi, w_lo = halves(np.kron(np.eye(2), basis_matrix()))
    t_hi, t_lo = w_hi.T, w_lo.T
    none = np.zeros_like(w_lo)
    forward = np.block([[t_hi, t_lo], [t_hi, none]])
    back_cols = np.block([[w_hi, w_lo], [w_hi, none]])
    back_rows = np.block([[t_hi, t_hi], [t_lo, none]])
    return forward, back_cols, back_rows


def split(x):
    hi = x.astype(BF)
    return hi, (x - hi.astype(F32)).astype(BF)


def mm(a, b):
    return jnp.dot(a, b, preferred_element_type=F32)


def mm_t(a, b):
    return lax.dot_general(a, b, (((1,), (1,)), ((), ())), preferred_element_type=F32)


def times(x, weights):
    both = mm(jnp.concatenate(split(x), axis=1), weights)
    return both[:, :128] + both[:, 128:]


def lane_tiles(x):
    return jnp.concatenate([x[:, j : j + 128] for j in range(0, x.shape[1], 128)], axis=0)


def back(grids, cols, rows):
    half = times(jnp.concatenate([lane_tiles(x) for x in grids], axis=0), cols)
    out = []
    for t in range(TILES):
        part = half[t * 256 : t * 256 + 256]
        hi, lo = split(jnp.concatenate([part[:128], part[128:]], axis=1))
        both = mm(rows, jnp.concatenate([hi, lo], axis=0))
        out.append(both[:128] + both[128:])
    return out


def lane_block(shape):
    return lax.shift_right_logical(lax.broadcasted_iota(jnp.int32, shape, len(shape) - 1), 5) & 3


def pick_kernel(m_hbm, g_hbm, idx_hbm, weights_hbm, v_ref, own_ref, mine_ref, theirs_ref, acc_ref, m_buf, g_buf, idx_buf, weights_ref, sems):
    p = lax.axis_index("dp")
    core = p & 1
    small = [
        pltpu.make_async_copy(weights_hbm, weights_ref, sems.at[0]),
        pltpu.make_async_copy(idx_hbm.at[pl.ds(p * BLOCKS, BLOCKS)], idx_buf, sems.at[1]),
    ]
    large = [
        (
            pltpu.make_async_copy(m_hbm.at[l], m_buf.at[l], sems.at[2 + 2 * l]),
            pltpu.make_async_copy(g_hbm.at[l], g_buf.at[l], sems.at[3 + 2 * l]),
        )
        for l in range(LAYERS)
    ]
    for copy in (*large[0], *small, *large[1], *large[2], *large[3]):
        copy.start()
    freq = lax.broadcasted_iota(jnp.int32, (GROUP, 128), 0)
    place = lax.broadcasted_iota(jnp.int32, (256, 256), 0)
    zeros = jnp.zeros((GROUP, 128), BF)

    def columns(l):
        acc = decay_rate * m_buf[l] + g_buf[l].astype(F32)
        acc_ref[l] = acc
        return times(lane_tiles(acc), weights_ref[...])

    def rows_and_pick(l, half):
        for t in range(TILES):
            turned = [half[u * 128 : u * 128 + 128].T for u in (2 * t, 2 * t + 1)]
            hi, lo = split(times(jnp.concatenate(turned, axis=0), weights_ref[...]))
            pos = [own_ref[pl.ds(l * 8 + a * 4 + t, 1), :] for a in range(2)]
            hot = [(freq == lax.shift_right_logical(x, 6)).astype(F32).astype(BF) for x in pos]
            pick = jnp.concatenate(
                [
                    jnp.concatenate([hot[0], zeros], axis=1),
                    jnp.concatenate([zeros, hot[1]], axis=1),
                ],
                axis=0,
            )
            got = mm(jnp.concatenate([hi, lo], axis=1), jnp.concatenate([pick, pick], axis=0))
            where = jnp.concatenate([(x & 63) + 64 * lane_block((1, 128)) for x in pos], axis=1)
            v = jnp.sum(jnp.where(place == where, got, 0.0), axis=0, keepdims=True)
            for a in range(2):
                v_ref[pl.ds(l * 8 + a * 4 + t, 1), :] = v[:, a * 128 : a * 128 + 128]

    def wait(l):
        for copy in large[l]:
            copy.wait()

    wait(0)
    for copy in small:
        copy.wait()
    own_ref[...] = jnp.concatenate([idx_buf[pl.ds(cj, 32, stride=4), :] for cj in range(4)], axis=1)
    rows_and_pick(0, columns(0))
    for l in range(1, LAYERS):
        wait(l)
    later = [columns(l) for l in range(1, LAYERS)]
    for l in range(1, LAYERS):
        rows_and_pick(l, later[l - 1])
    mine_ref[...] = v_ref[pl.ds(pl.multiple_of(core * 16, 16), 16), :]
    theirs_ref[...] = v_ref[pl.ds(pl.multiple_of(16 - core * 16, 16), 16), :]


def own_kernel(layers, acc_ref, own_ref, v_ref, cols_ref, rows_ref, *rest):
    out_hbm, out_buf, sems = rest[-3:]
    freq = lax.broadcasted_iota(jnp.int32, (GROUP, 128), 0)
    place = lax.broadcasted_iota(jnp.int32, (256, 128), 0)
    zeros = jnp.zeros((GROUP, 128), BF)
    copies = []
    for i, l in enumerate(layers):
        grids = []
        for t in range(TILES):
            left, right = [], []
            for a in range(2):
                row = l * 8 + a * 4 + t
                pos = own_ref[pl.ds(row, 1), :]
                v = v_ref[pl.ds(row, 1), :]
                left.append(split(jnp.where(freq == lax.shift_right_logical(pos, 6), v, 0.0)))
                right.append((place == (pos & 63) + 64 * lane_block((1, 128))).astype(F32).astype(BF))
            rows = []
            for h in range(2):
                rows.append(jnp.concatenate([left[0][h], zeros], axis=1))
                rows.append(jnp.concatenate([zeros, left[1][h]], axis=1))
            both = mm_t(jnp.concatenate(rows, axis=0), jnp.concatenate(right, axis=1))
            grids.append(both[:128] + both[128:])
        for t, tile in enumerate(back(grids, cols_ref[...], rows_ref[...])):
            s = slice(t * 256, t * 256 + 256)
            out_buf[i, :, s] = acc_ref[l, :, s] - tile
        copies.append(pltpu.make_async_copy(out_buf.at[i], out_hbm.at[l], sems.at[i]))
        copies[-1].start()
    for copy in copies:
        copy.wait()


def arrange_kernel(idx_ref, fr_ref, fc_ref):
    p = lax.axis_index("dp")
    half = BLOCKS // 2
    start = (p & 1) * half
    for q in range(REPLICAS // 4):
        pos = jnp.concatenate([idx_ref[pl.ds(pl.multiple_of((p ^ (4 * q + j)) * BLOCKS + start, half), half), :] for j in range(4)], axis=1)
        fr_ref[:, q * 128 : q * 128 + 128] = lax.shift_right_logical(pos, 6).astype(F32)
        fc_ref[:, q * 128 : q * 128 + 128] = (pos & 63).astype(F32)


def set_kernel(number, first, last, v_ref, fr_ref, fc_ref, *rest):
    old_ref = None
    if not first:
        old_ref, rest = rest[0], rest[1:]
    if last:
        grid_ref, sq_ref, val_ref = rest
        first_layer = (lax.axis_index("dp") & 1) * HALF
        sq_ref[...] = jnp.zeros_like(sq_ref)
    else:
        grid_ref, val_ref = rest
    lane = lane_block((16, 128))
    for q in range(SET // 4):
        x = [v_ref[4 * q + j] for j in range(4)]
        for cj in range(4):
            y = jnp.zeros((16, 128), F32)
            for j in range(4):
                moved = x[j] if j == cj else pltpu.roll(x[j], ((j - cj) * 32) % 128, 1)
                y = jnp.where(lane == j, moved, y)
            val_ref[cj, :, q * 128 : q * 128 + 128] = y
    wide = 32 * SET
    freq = lax.broadcasted_iota(jnp.int32, (GROUP, wide), 0).astype(F32).astype(BF)
    s = slice(number * wide, number * wide + wide)
    zero, one = jnp.zeros((), BF), jnp.ones((), BF)

    def body(l, carry):
        squares = jnp.zeros((1, 256), F32)
        for i in range(2 * TILES):
            a, t = i // TILES, i % TILES
            parts = []
            for cj in range(4):
                row = l * 32 + i * 4 + cj
                fr = fr_ref[pl.ds(row, 1), s].astype(BF)
                fc = fc_ref[pl.ds(row, 1), s].astype(BF)
                hi, lo = split(val_ref[cj, pl.ds(l * 8 + i, 1), :])
                at = freq == fr
                left = jnp.concatenate([jnp.where(at, hi, zero), jnp.where(at, lo, zero)], axis=0)
                both = mm_t(left, jnp.where(freq == fc, one, zero))
                parts.append(both[:GROUP] + both[GROUP:])
            grid = jnp.concatenate(parts, axis=1)
            if old_ref is not None:
                grid = grid + old_ref[l, t, a * GROUP : a * GROUP + GROUP, :]
            grid_ref[l, t, a * GROUP : a * GROUP + GROUP, :] = grid
            if last:
                squares = squares + jnp.sum(grid * grid, axis=0, keepdims=True)
        if last:
            sq_ref[pl.ds(first_layer + l, 1), :] = squares[:, :128] + squares[:, 128:]
        return carry

    for l in range(HALF):
        body(l, 0)


def decode_kernel(grid_ref, cols_ref, rows_ref, out_ref):
    def body(l, carry):
        tiles = back([grid_ref[l, t] for t in range(TILES)], cols_ref[...], rows_ref[...])
        for t, tile in enumerate(tiles):
            out_ref[l, :, t * 256 : t * 256 + 256] = tile
        return carry

    for l in range(HALF):
        body(l, 0)


def scale_kernel(mine_ref, theirs_ref, a_ref, b_ref, out_hbm, out_buf, factor_ref, sems):
    core = lax.axis_index("dp") & 1
    total = jnp.sum(a_ref[...] + b_ref[...], axis=1, keepdims=True)
    factor_ref[...] = lax.rsqrt(jnp.broadcast_to(total, (8, 128)) / ENTRIES + epsilon)
    copies = []
    for ref, start in ((mine_ref, core * HALF), (theirs_ref, HALF - core * HALF)):
        for i in range(HALF):
            l = start + i
            row = factor_ref[pl.ds(l, 1), :]
            for t in range(COLS // 128):
                s = slice(t * 128, t * 128 + 128)
                out_buf[l, :, s] = ref[i, :, s] * row
            copies.append(pltpu.make_async_copy(out_buf.at[l], out_hbm.at[l], sems.at[len(copies)]))
            copies[-1].start()
    for copy in copies:
        copy.wait()


VM = pl.BlockSpec(memory_space=pltpu.VMEM)
HB = pl.BlockSpec(memory_space=pltpu.HBM)
DECODED = jax.ShapeDtypeStruct((LAYERS, ROWS, COLS), F32)
GRIDS = jax.ShapeDtypeStruct((HALF, TILES, 128, 256), F32)
HALVED = jax.ShapeDtypeStruct((HALF, ROWS, COLS), F32)


def call(kernel, name, ins, outs, shapes, scratch=(), us=1.0, mib=32, **more):
    return pl.pallas_call(
        kernel,
        in_specs=ins,
        out_specs=outs,
        out_shape=shapes,
        scratch_shapes=list(scratch),
        compiler_params=pltpu.CompilerParams(vmem_limit_bytes=mib * 2**20),
        cost_estimate=pl.CostEstimate(flops=int(us * 1e9), bytes_accessed=int(us * 2e6), transcendentals=0),
        name=name,
        **more,
    )


def pick(m, g, idx, weights):
    return call(
        pick_kernel,
        "pick",
        [HB] * 4,
        [VM] * 5,
        [
            jax.ShapeDtypeStruct((32, 128), F32),
            jax.ShapeDtypeStruct((32, 128), jnp.int32),
            jax.ShapeDtypeStruct((16, 128), F32),
            jax.ShapeDtypeStruct((16, 128), F32),
            DECODED,
        ],
        [
            pltpu.VMEM((LAYERS, ROWS, COLS), F32),
            pltpu.VMEM((LAYERS, ROWS, COLS), BF),
            pltpu.VMEM((BLOCKS, TOPK), jnp.int32),
            pltpu.VMEM(weights.shape, BF),
            pltpu.SemaphoreType.DMA((2 + 2 * LAYERS,)),
        ],
        4.0,
    )(m, g, idx, weights)


def own_update(layers, acc, own, v, cols, rows, out=None):
    ins, more = [acc, own, v, cols, rows], {}
    if out is not None:
        ins.append(out)
        more = dict(input_output_aliases={5: 0})
    return call(
        lambda *refs: own_kernel(layers, *refs),
        f"own{layers[0]}",
        [VM] * 5 + [HB] * (len(ins) - 5),
        HB,
        DECODED,
        [pltpu.VMEM((len(layers), ROWS, COLS), F32), pltpu.SemaphoreType.DMA((len(layers),))],
        2.2,
        **more,
    )(*ins)


def arrange(idx):
    shape = jax.ShapeDtypeStruct((BLOCKS // 2, 1024), F32)
    return call(arrange_kernel, "arrange", [VM], [VM, VM], [shape, shape], (), 0.5)(idx)


def add_set(number, last, v, fr, fc, old):
    ins, outs, shapes, more = [v, fr, fc], [VM], [GRIDS], {}
    first = old is None
    if not first:
        ins.append(old)
        more = dict(input_output_aliases={3: 0})
    if last:
        outs.append(VM)
        shapes.append(jax.ShapeDtypeStruct((8, 128), F32))
    return call(
        lambda *refs: set_kernel(number, first, last, *refs),
        f"set{number}",
        [VM] * len(ins),
        outs,
        shapes,
        [pltpu.VMEM((4, 16, 32 * SET), F32)],
        1.6,
        **more,
    )(*ins)


def decode(grid, cols, rows):
    return call(decode_kernel, "decode", [VM] * 3, VM, HALVED, (), 1.6)(grid, cols, rows)


def rescale(mine, theirs, a, b):
    return call(
        scale_kernel,
        "rescale",
        [VM] * 4,
        HB,
        DECODED,
        [pltpu.VMEM((LAYERS, ROWS, COLS), F32), pltpu.VMEM((8, 128), F32), pltpu.SemaphoreType.DMA((LAYERS,))],
        1.0,
    )(mine, theirs, a, b)


def turn(x, axis, size, bit):
    return lax.ppermute(x, axis, [(i, i ^ bit) for i in range(size)])


def near_other_core(x):
    pairs = [(p * 8 + t, (p ^ 1) * 8 + (t ^ 1)) for p in range(REPLICAS) for t in range(8)]
    return lax.ppermute(x, ("dp", "tensor"), pairs)


def across(x):
    pairs = []
    for y in range(4):
        for z in range(8):
            for core in range(2):
                for tx in range(4):
                    to = (z + 6) % 8 if z in (0, 1, 4, 5) else (z + 2) % 8
                    place = [((y * 4 + k % 4) * 2 + core) * 8 + (k // 4) * 4 + tx for k in (z, to)]
                    pairs.append(tuple(place))
    return lax.ppermute(x, ("dp", "tensor"), pairs)


def on_device(momentum, gradient, kept_index):
    m, g = momentum[0], gradient[0]
    idx = kept_index.reshape(REPLICAS * BLOCKS, TOPK)
    forward, back_cols, back_rows = (jnp.asarray(x) for x in constants())
    held = [pltpu.with_memory_space_constraint(x, pltpu.HBM) for x in (m, g, idx, forward)]
    v, own, mine, theirs, acc = pick(*held)

    x = jnp.stack([mine, turn(theirs, "dp", REPLICAS, 1)])
    x, v, idx = lax.optimization_barrier((x, v, idx))
    x = jnp.concatenate([x] + [turn(x, "dp", REPLICAS, b) for b in (2, 4, 6)], axis=0)
    fr, fc = arrange(idx)
    momentum_out = own_update((0, 1), acc, own, v, back_cols, back_rows)
    x, momentum_out = lax.optimization_barrier((x, momentum_out))
    order = (0, 1, 3, 2)
    sets = {s: x if s == 0 else turn(x, "dp", REPLICAS, 8 * s) for s in order}
    grid = None
    for s in order[:-1]:
        (grid,) = add_set(s, False, sets[s], fr, fc, grid)
    grid, squares = add_set(order[-1], True, sets[order[-1]], fr, fc, grid)

    other_grid = turn(grid, "dp", REPLICAS, 1)
    beside = turn(squares, "dp", REPLICAS, 1)
    near = turn(squares, "tensor", 8, 1)
    across_near = near_other_core(squares)
    squares, v = lax.optimization_barrier((squares, v))
    momentum_out = own_update((2, 3), acc, own, v, back_cols, back_rows, momentum_out)
    decoded = decode(grid, back_cols, back_rows)
    other = decode(other_grid, back_cols, back_rows)
    total = squares + beside + near + across_near
    total = total + turn(total, "tensor", 8, 3)
    update = rescale(decoded, other, total, across(total))
    return (momentum_out[None], update)


def solution(mesh):
    placed = (
        P("dp", None, None, "tensor"),
        P("dp", None, None, "tensor"),
        P(None, None, None, "tensor", None),
    )
    return jax.shard_map(
        on_device,
        mesh=mesh,
        in_specs=placed,
        out_specs=(P("dp", None, None, "tensor"), P(None, None, "tensor")),
        check_vma=False,
    )
```

```python
import math

import jax
import jax.numpy as jnp
import ml_dtypes
import numpy as np
from jax import lax
from jax.experimental import pallas as pl
from jax.experimental.pallas import tpu as pltpu
from jax.sharding import PartitionSpec as P

GROUP = 64
TOPK = 32
REPLICAS = 32
LAYERS = 4
ROWS = 128
COLS = 1024
TILES = COLS // 256
BLOCKS = 128
SET = 8
ENTRIES = 128 * 8192
HALF = LAYERS // 2

decay_rate = 0.999
epsilon = 1e-06

BF = jnp.bfloat16
F32 = jnp.float32


def basis_matrix():
    f = np.arange(GROUP, dtype=np.float64)[:, None]
    n = np.arange(GROUP, dtype=np.float64)[None, :]
    scale = np.where(f == 0, math.sqrt(1.0 / GROUP), math.sqrt(2.0 / GROUP))
    return scale * np.cos(math.pi * (2.0 * n + 1.0) * f / (2.0 * GROUP))


def halves(x):
    x = x.astype(np.float32)
    hi = x.astype(ml_dtypes.bfloat16)
    lo = (x - hi.astype(np.float32)).astype(ml_dtypes.bfloat16)
    return hi, lo


def constants():
    w_hi, w_lo = halves(np.kron(np.eye(2), basis_matrix()))
    t_hi, t_lo = w_hi.T, w_lo.T
    none = np.zeros_like(w_lo)
    forward = np.block([[t_hi, t_lo], [t_hi, none]])
    back_cols = np.block([[w_hi, w_lo], [w_hi, none]])
    back_rows = np.block([[t_hi, t_hi], [t_lo, none]])
    return forward, back_cols, back_rows


def split(x):
    hi = x.astype(BF)
    return hi, (x - hi.astype(F32)).astype(BF)


def mm(a, b):
    return jnp.dot(a, b, preferred_element_type=F32)


def mm_t(a, b):
    return lax.dot_general(a, b, (((1,), (1,)), ((), ())), preferred_element_type=F32)


def times(x, weights):
    both = mm(jnp.concatenate(split(x), axis=1), weights)
    return both[:, :128] + both[:, 128:]


def lane_tiles(x):
    return jnp.concatenate([x[:, j : j + 128] for j in range(0, x.shape[1], 128)], axis=0)


def back(grids, cols, rows):
    half = times(jnp.concatenate([lane_tiles(x) for x in grids], axis=0), cols)
    out = []
    for t in range(TILES):
        part = half[t * 256 : t * 256 + 256]
        hi, lo = split(jnp.concatenate([part[:128], part[128:]], axis=1))
        both = mm(rows, jnp.concatenate([hi, lo], axis=0))
        out.append(both[:128] + both[128:])
    return out


def lane_block(shape):
    return lax.shift_right_logical(lax.broadcasted_iota(jnp.int32, shape, len(shape) - 1), 5) & 3


def columns(acc, weights):
    return times(lane_tiles(acc), weights)


def rows_and_pick(half, weights, pos_ref, row, v_ref, to):
    freq = lax.broadcasted_iota(jnp.int32, (GROUP, 128), 0)
    place = lax.broadcasted_iota(jnp.int32, (256, 256), 0)
    zeros = jnp.zeros((GROUP, 128), BF)
    for t in range(TILES):
        turned = [half[u * 128 : u * 128 + 128].T for u in (2 * t, 2 * t + 1)]
        hi, lo = split(times(jnp.concatenate(turned, axis=0), weights))
        pos = [pos_ref[pl.ds(row + a * 4 + t, 1), :] for a in range(2)]
        hot = [(freq == lax.shift_right_logical(x, 6)).astype(F32).astype(BF) for x in pos]
        pick = jnp.concatenate(
            [
                jnp.concatenate([hot[0], zeros], axis=1),
                jnp.concatenate([zeros, hot[1]], axis=1),
            ],
            axis=0,
        )
        got = mm(jnp.concatenate([hi, lo], axis=1), jnp.concatenate([pick, pick], axis=0))
        where = jnp.concatenate([(x & 63) + 64 * lane_block((1, 128)) for x in pos], axis=1)
        v = jnp.sum(jnp.where(place == where, got, 0.0), axis=0, keepdims=True)
        for a in range(2):
            v_ref[pl.ds(to + a * 4 + t, 1), :] = v[:, a * 128 : a * 128 + 128]


def theirs_kernel(m_hbm, g_hbm, idx_hbm, weights_hbm, v_ref, pos_ref, acc_ref, m_buf, g_buf, idx_buf, all_ref, weights_ref, sems):
    p = lax.axis_index("dp")
    core = p & 1
    order = [HALF - HALF * core + i for i in range(HALF)] + [HALF * core + i for i in range(HALF)]
    small = [
        pltpu.make_async_copy(weights_hbm, weights_ref, sems.at[0]),
        pltpu.make_async_copy(idx_hbm.at[pl.ds(p * BLOCKS, BLOCKS)], idx_buf, sems.at[1]),
    ]
    large = [
        (
            pltpu.make_async_copy(m_hbm.at[l], m_buf.at[i], sems.at[2 + 2 * i]),
            pltpu.make_async_copy(g_hbm.at[l], g_buf.at[i], sems.at[3 + 2 * i]),
        )
        for i, l in enumerate(order)
    ]
    for copy in (*large[0], *small, *large[1], *large[2], *large[3]):
        copy.start()

    def accumulate(i):
        acc = decay_rate * m_buf[i] + g_buf[i].astype(F32)
        acc_ref[i] = acc
        return acc

    def wait(i):
        for copy in large[i]:
            copy.wait()

    wait(0)
    for copy in small:
        copy.wait()
    all_ref[...] = jnp.concatenate([idx_buf[pl.ds(cj, 32, stride=4), :] for cj in range(4)], axis=1)
    pos_ref[:16] = all_ref[pl.ds(pl.multiple_of(16 - core * 16, 16), 16), :]
    pos_ref[16:] = all_ref[pl.ds(pl.multiple_of(core * 16, 16), 16), :]
    rows_and_pick(columns(accumulate(0), weights_ref[...]), weights_ref[...], pos_ref, 0, v_ref, 0)
    for i in range(1, LAYERS):
        wait(i)
    rows_and_pick(columns(accumulate(1), weights_ref[...]), weights_ref[...], pos_ref, 8, v_ref, 8)
    for i in range(HALF, LAYERS):
        accumulate(i)


def mine_kernel(acc_ref, pos_ref, weights_ref, v_ref):
    halves_of = [columns(acc_ref[HALF + i], weights_ref[...]) for i in range(HALF)]
    for i in range(HALF):
        rows_and_pick(halves_of[i], weights_ref[...], pos_ref, 16 + 8 * i, v_ref, 8 * i)


def own_kernel(which, acc_ref, own_ref, v_ref, cols_ref, rows_ref, *rest):
    out_hbm, out_buf, sems = rest[-3:]
    freq = lax.broadcasted_iota(jnp.int32, (GROUP, 128), 0)
    place = lax.broadcasted_iota(jnp.int32, (256, 128), 0)
    zeros = jnp.zeros((GROUP, 128), BF)
    copies = []
    core = lax.axis_index("dp") & 1
    start = HALF - HALF * core if which == 0 else HALF * core
    for i in range(HALF):
        l = which * HALF + i
        grids = []
        for t in range(TILES):
            left, right = [], []
            for a in range(2):
                row = l * 8 + a * 4 + t
                pos = own_ref[pl.ds(row, 1), :]
                v = v_ref[pl.ds(i * 8 + a * 4 + t, 1), :]
                left.append(split(jnp.where(freq == lax.shift_right_logical(pos, 6), v, 0.0)))
                right.append((place == (pos & 63) + 64 * lane_block((1, 128))).astype(F32).astype(BF))
            rows = []
            for h in range(2):
                rows.append(jnp.concatenate([left[0][h], zeros], axis=1))
                rows.append(jnp.concatenate([zeros, left[1][h]], axis=1))
            both = mm_t(jnp.concatenate(rows, axis=0), jnp.concatenate(right, axis=1))
            grids.append(both[:128] + both[128:])
        for t, tile in enumerate(back(grids, cols_ref[...], rows_ref[...])):
            s = slice(t * 256, t * 256 + 256)
            out_buf[i, :, s] = acc_ref[l, :, s] - tile
        copies.append(pltpu.make_async_copy(out_buf.at[i], out_hbm.at[start + i], sems.at[i]))
        copies[-1].start()
    for copy in copies:
        copy.wait()


def arrange_kernel(idx_ref, fr_ref, fc_ref):
    p = lax.axis_index("dp")
    half = BLOCKS // 2
    start = (p & 1) * half
    for q in range(REPLICAS // 4):
        pos = jnp.concatenate([idx_ref[pl.ds(pl.multiple_of((p ^ (4 * q + j)) * BLOCKS + start, half), half), :] for j in range(4)], axis=1)
        fr_ref[:, q * 128 : q * 128 + 128] = lax.shift_right_logical(pos, 6).astype(F32)
        fc_ref[:, q * 128 : q * 128 + 128] = (pos & 63).astype(F32)


def set_kernel(places, first, last, *rest):
    v_refs, (fr_ref, fc_ref), rest = rest[: len(places)], rest[len(places) : len(places) + 2], rest[len(places) + 2 :]
    old_ref = None
    if not first:
        old_ref, rest = rest[0], rest[1:]
    if last:
        grid_ref, sq_ref, val_ref = rest
        first_layer = (lax.axis_index("dp") & 1) * HALF
        sq_ref[...] = jnp.zeros_like(sq_ref)
    else:
        grid_ref, val_ref = rest
    lane = lane_block((16, 128))
    for n, v_ref in enumerate(v_refs):
        for q in range(SET // 4):
            x = [v_ref[4 * q + j] for j in range(4)]
            for cj in range(4):
                y = jnp.zeros((16, 128), F32)
                for j in range(4):
                    moved = x[j] if j == cj else pltpu.roll(x[j], ((j - cj) * 32) % 128, 1)
                    y = jnp.where(lane == j, moved, y)
                start = (n * SET // 4 + q) * 128
                val_ref[cj, :, start : start + 128] = y
    wide = 32 * SET
    freq = lax.broadcasted_iota(jnp.int32, (GROUP, wide), 0).astype(F32).astype(BF)
    zero, one = jnp.zeros((), BF), jnp.ones((), BF)
    for l in range(HALF):
        squares = jnp.zeros((1, 256), F32)
        for i in range(2 * TILES):
            a, t = i // TILES, i % TILES
            parts = []
            for cj in range(4):
                row = l * 32 + i * 4 + cj
                left, right = [], []
                for n, place in enumerate(places):
                    s = slice(place * wide, place * wide + wide)
                    fr = fr_ref[pl.ds(row, 1), s].astype(BF)
                    fc = fc_ref[pl.ds(row, 1), s].astype(BF)
                    hi, lo = split(val_ref[cj, pl.ds(l * 8 + i, 1), n * wide : n * wide + wide])
                    at = freq == fr
                    left.append(jnp.concatenate([jnp.where(at, hi, zero), jnp.where(at, lo, zero)], axis=0))
                    right.append(jnp.where(freq == fc, one, zero))
                both = mm_t(jnp.concatenate(left, axis=1), jnp.concatenate(right, axis=1))
                parts.append(both[:GROUP] + both[GROUP:])
            grid = jnp.concatenate(parts, axis=1)
            if old_ref is not None:
                grid = grid + old_ref[l, t, a * GROUP : a * GROUP + GROUP, :]
            grid_ref[l, t, a * GROUP : a * GROUP + GROUP, :] = grid
            if last:
                squares = squares + jnp.sum(grid * grid, axis=0, keepdims=True)
        if last:
            sq_ref[pl.ds(first_layer + l, 1), :] = squares[:, :128] + squares[:, 128:]


def decode_kernel(grid_ref, cols_ref, rows_ref, out_ref):
    def body(l, carry):
        tiles = back([grid_ref[l, t] for t in range(TILES)], cols_ref[...], rows_ref[...])
        for t, tile in enumerate(tiles):
            out_ref[l, :, t * 256 : t * 256 + 256] = tile
        return carry

    for l in range(HALF):
        body(l, 0)


def scale_kernel(mine_ref, theirs_ref, a_ref, b_ref, out_hbm, out_buf, factor_ref, sems):
    core = lax.axis_index("dp") & 1
    total = jnp.sum(a_ref[...] + b_ref[...], axis=1, keepdims=True)
    factor_ref[...] = lax.rsqrt(jnp.broadcast_to(total, (8, 128)) / ENTRIES + epsilon)
    copies = []
    for ref, start in ((mine_ref, core * HALF), (theirs_ref, HALF - core * HALF)):
        for i in range(HALF):
            l = start + i
            row = factor_ref[pl.ds(l, 1), :]
            for t in range(COLS // 128):
                s = slice(t * 128, t * 128 + 128)
                out_buf[l, :, s] = ref[i, :, s] * row
            copies.append(pltpu.make_async_copy(out_buf.at[l], out_hbm.at[l], sems.at[len(copies)]))
            copies[-1].start()
    for copy in copies:
        copy.wait()


VM = pl.BlockSpec(memory_space=pltpu.VMEM)
HB = pl.BlockSpec(memory_space=pltpu.HBM)
DECODED = jax.ShapeDtypeStruct((LAYERS, ROWS, COLS), F32)
GRIDS = jax.ShapeDtypeStruct((HALF, TILES, 128, 256), F32)
HALVED = jax.ShapeDtypeStruct((HALF, ROWS, COLS), F32)


def call(kernel, name, ins, outs, shapes, scratch=(), us=1.0, mib=32, **more):
    return pl.pallas_call(
        kernel,
        in_specs=ins,
        out_specs=outs,
        out_shape=shapes,
        scratch_shapes=list(scratch),
        compiler_params=pltpu.CompilerParams(vmem_limit_bytes=mib * 2**20),
        cost_estimate=pl.CostEstimate(flops=int(us * 1e9), bytes_accessed=int(us * 2e6), transcendentals=0),
        name=name,
        **more,
    )


def pick_theirs(m, g, idx, weights):
    return call(
        theirs_kernel,
        "theirs",
        [HB] * 4,
        [VM] * 3,
        [
            jax.ShapeDtypeStruct((16, 128), F32),
            jax.ShapeDtypeStruct((32, 128), jnp.int32),
            DECODED,
        ],
        [
            pltpu.VMEM((LAYERS, ROWS, COLS), F32),
            pltpu.VMEM((LAYERS, ROWS, COLS), BF),
            pltpu.VMEM((BLOCKS, TOPK), jnp.int32),
            pltpu.VMEM((32, 128), jnp.int32),
            pltpu.VMEM(weights.shape, BF),
            pltpu.SemaphoreType.DMA((2 + 2 * LAYERS,)),
        ],
        2.5,
    )(m, g, idx, weights)


def pick_mine(acc, pos, weights):
    return call(mine_kernel, "mine", [VM] * 3, VM, jax.ShapeDtypeStruct((16, 128), F32), (), 1.7)(acc, pos, weights)


def own_update(which, acc, pos, v, cols, rows, out=None):
    ins, more = [acc, pos, v, cols, rows], {}
    if out is not None:
        ins.append(out)
        more = dict(input_output_aliases={5: 0})
    return call(
        lambda *refs: own_kernel(which, *refs),
        f"own{which}",
        [VM] * 5 + [HB] * (len(ins) - 5),
        HB,
        DECODED,
        [pltpu.VMEM((HALF, ROWS, COLS), F32), pltpu.SemaphoreType.DMA((HALF,))],
        2.2,
        **more,
    )(*ins)


def arrange(idx):
    shape = jax.ShapeDtypeStruct((BLOCKS // 2, 1024), F32)
    return call(arrange_kernel, "arrange", [VM], [VM, VM], [shape, shape], (), 0.5)(idx)


def add_sets(places, last, sets, fr, fc, old):
    ins, outs, shapes, more = [*(sets[s] for s in places), fr, fc], [VM], [GRIDS], {}
    first = old is None
    if not first:
        more = dict(input_output_aliases={len(ins): 0})
        ins.append(old)
    if last:
        outs.append(VM)
        shapes.append(jax.ShapeDtypeStruct((8, 128), F32))
    return call(
        lambda *refs: set_kernel(places, first, last, *refs),
        "sets" + "".join(str(s) for s in places),
        [VM] * len(ins),
        outs,
        shapes,
        [pltpu.VMEM((4, 16, 32 * SET * len(places)), F32)],
        1.4 * len(places),
        **more,
    )(*ins)


def decode(grid, cols, rows):
    return call(decode_kernel, "decode", [VM] * 3, VM, HALVED, (), 1.6)(grid, cols, rows)


def rescale(mine, theirs, a, b):
    return call(
        scale_kernel,
        "rescale",
        [VM] * 4,
        HB,
        DECODED,
        [pltpu.VMEM((LAYERS, ROWS, COLS), F32), pltpu.VMEM((8, 128), F32), pltpu.SemaphoreType.DMA((LAYERS,))],
        1.0,
    )(mine, theirs, a, b)


def turn(x, axis, size, bit):
    return lax.ppermute(x, axis, [(i, i ^ bit) for i in range(size)])


def near_other_core(x):
    pairs = [(p * 8 + t, (p ^ 1) * 8 + (t ^ 1)) for p in range(REPLICAS) for t in range(8)]
    return lax.ppermute(x, ("dp", "tensor"), pairs)


def across(x):
    pairs = []
    for y in range(4):
        for z in range(8):
            for core in range(2):
                for tx in range(4):
                    to = (z + 6) % 8 if z in (0, 1, 4, 5) else (z + 2) % 8
                    place = [((y * 4 + k % 4) * 2 + core) * 8 + (k // 4) * 4 + tx for k in (z, to)]
                    pairs.append(tuple(place))
    return lax.ppermute(x, ("dp", "tensor"), pairs)


def on_device(momentum, gradient, kept_index):
    m, g = momentum[0], gradient[0]
    idx = kept_index.reshape(REPLICAS * BLOCKS, TOPK)
    forward, back_cols, back_rows = (jnp.asarray(x) for x in constants())
    held = [pltpu.with_memory_space_constraint(x, pltpu.HBM) for x in (m, g, idx, forward)]
    theirs, pos, acc = pick_theirs(*held)
    mine = pick_mine(acc, pos, forward)

    x = jnp.stack([mine, turn(theirs, "dp", REPLICAS, 1)])
    x, theirs, idx = lax.optimization_barrier((x, theirs, idx))
    x = jnp.concatenate([x] + [turn(x, "dp", REPLICAS, b) for b in (2, 4, 6)], axis=0)
    fr, fc = arrange(idx)
    momentum_out = own_update(0, acc, pos, theirs, back_cols, back_rows)
    x, momentum_out = lax.optimization_barrier((x, momentum_out))
    calls = ((0,), (1,), (3,), (2,))
    sets = {s: x if s == 0 else turn(x, "dp", REPLICAS, 8 * s) for c in calls for s in c}
    grid = None
    for places in calls[:-1]:
        (grid,) = add_sets(places, False, sets, fr, fc, grid)
    grid, squares = add_sets(calls[-1], True, sets, fr, fc, grid)

    other_grid = turn(grid, "dp", REPLICAS, 1)
    beside = turn(squares, "dp", REPLICAS, 1)
    near = turn(squares, "tensor", 8, 1)
    across_near = near_other_core(squares)
    squares, mine = lax.optimization_barrier((squares, mine))
    momentum_out = own_update(1, acc, pos, mine, back_cols, back_rows, momentum_out)
    decoded = decode(grid, back_cols, back_rows)
    other = decode(other_grid, back_cols, back_rows)
    total = squares + beside + near + across_near
    total = total + turn(total, "tensor", 8, 3)
    update = rescale(decoded, other, total, across(total))
    return (momentum_out[None], update)


def solution(mesh):
    placed = (
        P("dp", None, None, "tensor"),
        P("dp", None, None, "tensor"),
        P(None, None, None, "tensor", None),
    )
    return jax.shard_map(
        on_device,
        mesh=mesh,
        in_specs=placed,
        out_specs=(P("dp", None, None, "tensor"), P(None, None, "tensor")),
        check_vma=False,
    )
```

```python
import math

import jax
import jax.numpy as jnp
import ml_dtypes
import numpy as np
from jax import lax
from jax.experimental import pallas as pl
from jax.experimental.pallas import tpu as pltpu
from jax.sharding import PartitionSpec as P

GROUP = 64
TOPK = 32
REPLICAS = 32
LAYERS = 4
ROWS = 128
COLS = 1024
TILES = COLS // 256
BLOCKS = 128
SET = 8
ENTRIES = 128 * 8192
HALF = LAYERS // 2

decay_rate = 0.999
epsilon = 1e-06

BF = jnp.bfloat16
F32 = jnp.float32


def basis_matrix():
    f = np.arange(GROUP, dtype=np.float64)[:, None]
    n = np.arange(GROUP, dtype=np.float64)[None, :]
    scale = np.where(f == 0, math.sqrt(1.0 / GROUP), math.sqrt(2.0 / GROUP))
    return scale * np.cos(math.pi * (2.0 * n + 1.0) * f / (2.0 * GROUP))


def halves(x):
    x = x.astype(np.float32)
    hi = x.astype(ml_dtypes.bfloat16)
    lo = (x - hi.astype(np.float32)).astype(ml_dtypes.bfloat16)
    return hi, lo


def constants():
    w_hi, w_lo = halves(np.kron(np.eye(2), basis_matrix()))
    t_hi, t_lo = w_hi.T, w_lo.T
    none = np.zeros_like(w_lo)
    forward = np.block([[t_hi, t_lo], [t_hi, none]])
    back_cols = np.block([[w_hi, w_lo], [w_hi, none]])
    back_rows = np.block([[t_hi, t_hi], [t_lo, none]])
    return forward, back_cols, back_rows


def split(x):
    hi = x.astype(BF)
    return hi, (x - hi.astype(F32)).astype(BF)


def mm(a, b):
    return jnp.dot(a, b, preferred_element_type=F32)


def mm_t(a, b):
    return lax.dot_general(a, b, (((1,), (1,)), ((), ())), preferred_element_type=F32)


def times(x, weights):
    both = mm(jnp.concatenate(split(x), axis=1), weights)
    return both[:, :128] + both[:, 128:]


def lane_tiles(x):
    return jnp.concatenate([x[:, j : j + 128] for j in range(0, x.shape[1], 128)], axis=0)


def back(grids, cols, rows):
    half = times(jnp.concatenate([lane_tiles(x) for x in grids], axis=0), cols)
    out = []
    for t in range(TILES):
        part = half[t * 256 : t * 256 + 256]
        hi, lo = split(jnp.concatenate([part[:128], part[128:]], axis=1))
        both = mm(rows, jnp.concatenate([hi, lo], axis=0))
        out.append(both[:128] + both[128:])
    return out


def lane_block(shape):
    return lax.shift_right_logical(lax.broadcasted_iota(jnp.int32, shape, len(shape) - 1), 5) & 3


def columns(acc, weights):
    return times(lane_tiles(acc), weights)


def rows_and_pick(half, weights, pos_ref, row, v_ref, to):
    freq = lax.broadcasted_iota(jnp.int32, (GROUP, 128), 0)
    place = lax.broadcasted_iota(jnp.int32, (256, 256), 0)
    zeros = jnp.zeros((GROUP, 128), BF)
    for t in range(TILES):
        turned = [half[u * 128 : u * 128 + 128].T for u in (2 * t, 2 * t + 1)]
        hi, lo = split(times(jnp.concatenate(turned, axis=0), weights))
        pos = [pos_ref[pl.ds(row + a * 4 + t, 1), :] for a in range(2)]
        hot = [(freq == lax.shift_right_logical(x, 6)).astype(F32).astype(BF) for x in pos]
        pick = jnp.concatenate(
            [
                jnp.concatenate([hot[0], zeros], axis=1),
                jnp.concatenate([zeros, hot[1]], axis=1),
            ],
            axis=0,
        )
        got = mm(jnp.concatenate([hi, lo], axis=1), jnp.concatenate([pick, pick], axis=0))
        where = jnp.concatenate([(x & 63) + 64 * lane_block((1, 128)) for x in pos], axis=1)
        v = jnp.sum(jnp.where(place == where, got, 0.0), axis=0, keepdims=True)
        for a in range(2):
            v_ref[pl.ds(to + a * 4 + t, 1), :] = v[:, a * 128 : a * 128 + 128]


def theirs_kernel(m_hbm, g_hbm, idx_hbm, weights_hbm, v_ref, pos_ref, acc_ref, m_buf, g_buf, idx_buf, all_ref, weights_ref, sems):
    p = lax.axis_index("dp")
    core = p & 1
    order = [HALF - HALF * core + i for i in range(HALF)] + [HALF * core + i for i in range(HALF)]
    small = [
        pltpu.make_async_copy(weights_hbm, weights_ref, sems.at[0]),
        pltpu.make_async_copy(idx_hbm.at[pl.ds(p * BLOCKS, BLOCKS)], idx_buf, sems.at[1]),
    ]
    large = [
        (
            pltpu.make_async_copy(m_hbm.at[l], m_buf.at[i], sems.at[2 + 2 * i]),
            pltpu.make_async_copy(g_hbm.at[l], g_buf.at[i], sems.at[3 + 2 * i]),
        )
        for i, l in enumerate(order)
    ]
    for copy in (*large[0], *small, *large[1], *large[2], *large[3]):
        copy.start()

    def accumulate(i):
        acc = decay_rate * m_buf[i] + g_buf[i].astype(F32)
        acc_ref[i] = acc
        return acc

    def wait(i):
        for copy in large[i]:
            copy.wait()

    wait(0)
    for copy in small:
        copy.wait()
    all_ref[...] = jnp.concatenate([idx_buf[pl.ds(cj, 32, stride=4), :] for cj in range(4)], axis=1)
    pos_ref[:16] = all_ref[pl.ds(pl.multiple_of(16 - core * 16, 16), 16), :]
    pos_ref[16:] = all_ref[pl.ds(pl.multiple_of(core * 16, 16), 16), :]
    rows_and_pick(columns(accumulate(0), weights_ref[...]), weights_ref[...], pos_ref, 0, v_ref, 0)
    for i in range(1, LAYERS):
        wait(i)
    rows_and_pick(columns(accumulate(1), weights_ref[...]), weights_ref[...], pos_ref, 8, v_ref, 8)
    for i in range(HALF, LAYERS):
        accumulate(i)


def mine_kernel(acc_ref, pos_ref, weights_ref, v_ref):
    halves_of = [columns(acc_ref[HALF + i], weights_ref[...]) for i in range(HALF)]
    for i in range(HALF):
        rows_and_pick(halves_of[i], weights_ref[...], pos_ref, 16 + 8 * i, v_ref, 8 * i)


def own_kernel(which, acc_ref, own_ref, v_ref, cols_ref, rows_ref, *rest):
    out_hbm, out_buf, sems = rest[-3:]
    freq = lax.broadcasted_iota(jnp.int32, (GROUP, 128), 0)
    place = lax.broadcasted_iota(jnp.int32, (256, 128), 0)
    zeros = jnp.zeros((GROUP, 128), BF)
    copies = []
    core = lax.axis_index("dp") & 1
    start = HALF - HALF * core if which == 0 else HALF * core
    for i in range(HALF):
        l = which * HALF + i
        grids = []
        for t in range(TILES):
            left, right = [], []
            for a in range(2):
                row = l * 8 + a * 4 + t
                pos = own_ref[pl.ds(row, 1), :]
                v = v_ref[pl.ds(i * 8 + a * 4 + t, 1), :]
                left.append(split(jnp.where(freq == lax.shift_right_logical(pos, 6), v, 0.0)))
                right.append((place == (pos & 63) + 64 * lane_block((1, 128))).astype(F32).astype(BF))
            rows = []
            for h in range(2):
                rows.append(jnp.concatenate([left[0][h], zeros], axis=1))
                rows.append(jnp.concatenate([zeros, left[1][h]], axis=1))
            both = mm_t(jnp.concatenate(rows, axis=0), jnp.concatenate(right, axis=1))
            grids.append(both[:128] + both[128:])
        for t, tile in enumerate(back(grids, cols_ref[...], rows_ref[...])):
            s = slice(t * 256, t * 256 + 256)
            out_buf[i, :, s] = acc_ref[l, :, s] - tile
        copies.append(pltpu.make_async_copy(out_buf.at[i], out_hbm.at[start + i], sems.at[i]))
        copies[-1].start()
    for copy in copies:
        copy.wait()


def arrange_kernel(idx_ref, fr_ref, fc_ref):
    p = lax.axis_index("dp")
    half = BLOCKS // 2
    start = (p & 1) * half
    for q in range(REPLICAS // 4):
        pos = jnp.concatenate([idx_ref[pl.ds(pl.multiple_of((p ^ (4 * q + j)) * BLOCKS + start, half), half), :] for j in range(4)], axis=1)
        fr_ref[:, q * 128 : q * 128 + 128] = lax.shift_right_logical(pos, 6).astype(F32)
        fc_ref[:, q * 128 : q * 128 + 128] = (pos & 63).astype(F32)


def set_kernel(places, first, last, *rest):
    v_refs, (fr_ref, fc_ref), rest = rest[: len(places)], rest[len(places) : len(places) + 2], rest[len(places) + 2 :]
    old_ref = None
    if not first:
        old_ref, rest = rest[0], rest[1:]
    if last:
        grid_ref, sq_ref, val_ref = rest
        first_layer = (lax.axis_index("dp") & 1) * HALF
        sq_ref[...] = jnp.zeros_like(sq_ref)
    else:
        grid_ref, val_ref = rest
    lane = lane_block((16, 128))
    for n, v_ref in enumerate(v_refs):
        for q in range(SET // 4):
            x = [v_ref[4 * q + j] for j in range(4)]
            for cj in range(4):
                y = jnp.zeros((16, 128), F32)
                for j in range(4):
                    moved = x[j] if j == cj else pltpu.roll(x[j], ((j - cj) * 32) % 128, 1)
                    y = jnp.where(lane == j, moved, y)
                start = (n * SET // 4 + q) * 128
                val_ref[cj, :, start : start + 128] = y
    wide = 32 * SET
    freq = lax.broadcasted_iota(jnp.int32, (GROUP, wide), 0).astype(F32).astype(BF)
    zero, one = jnp.zeros((), BF), jnp.ones((), BF)
    for l in range(HALF):
        squares = jnp.zeros((1, 256), F32)
        for i in range(2 * TILES):
            a, t = i // TILES, i % TILES
            parts = []
            for cj in range(4):
                row = l * 32 + i * 4 + cj
                left, right = [], []
                for n, place in enumerate(places):
                    s = slice(place * wide, place * wide + wide)
                    fr = fr_ref[pl.ds(row, 1), s].astype(BF)
                    fc = fc_ref[pl.ds(row, 1), s].astype(BF)
                    hi, lo = split(val_ref[cj, pl.ds(l * 8 + i, 1), n * wide : n * wide + wide])
                    at = freq == fr
                    left.append(jnp.concatenate([jnp.where(at, hi, zero), jnp.where(at, lo, zero)], axis=0))
                    right.append(jnp.where(freq == fc, one, zero))
                both = mm_t(jnp.concatenate(left, axis=1), jnp.concatenate(right, axis=1))
                parts.append(both[:GROUP] + both[GROUP:])
            grid = jnp.concatenate(parts, axis=1)
            if old_ref is not None:
                grid = grid + old_ref[l, t, a * GROUP : a * GROUP + GROUP, :]
            grid_ref[l, t, a * GROUP : a * GROUP + GROUP, :] = grid
            if last:
                squares = squares + jnp.sum(grid * grid, axis=0, keepdims=True)
        if last:
            sq_ref[pl.ds(first_layer + l, 1), :] = squares[:, :128] + squares[:, 128:]


def decode_kernel(grid_ref, cols_ref, rows_ref, out_ref):
    def body(l, carry):
        tiles = back([grid_ref[l, t] for t in range(TILES)], cols_ref[...], rows_ref[...])
        for t, tile in enumerate(tiles):
            out_ref[l, :, t * 256 : t * 256 + 256] = tile
        return carry

    for l in range(HALF):
        body(l, 0)


def scale_kernel(again, mine_ref, theirs_ref, total_ref, *rest):
    out_hbm, out_buf, factor_ref, sems = rest[-4:]
    core = lax.axis_index("dp") & 1

    def scale():
        total = jnp.sum(total_ref[...], axis=1, keepdims=True)
        factor_ref[...] = lax.rsqrt(jnp.broadcast_to(total, (8, 128)) / ENTRIES + epsilon)
        copies = []
        for ref, start in ((mine_ref, core * HALF), (theirs_ref, HALF - core * HALF)):
            for i in range(HALF):
                l = start + i
                row = factor_ref[pl.ds(l, 1), :]
                for t in range(COLS // 128):
                    s = slice(t * 128, t * 128 + 128)
                    out_buf[l, :, s] = ref[i, :, s] * row
                copies.append(pltpu.make_async_copy(out_buf.at[l], out_hbm.at[l], sems.at[len(copies)]))
                copies[-1].start()
        for copy in copies:
            copy.wait()

    if again:
        pl.when(core == 0)(scale)
    else:
        scale()


VM = pl.BlockSpec(memory_space=pltpu.VMEM)
HB = pl.BlockSpec(memory_space=pltpu.HBM)
DECODED = jax.ShapeDtypeStruct((LAYERS, ROWS, COLS), F32)
GRIDS = jax.ShapeDtypeStruct((HALF, TILES, 128, 256), F32)
HALVED = jax.ShapeDtypeStruct((HALF, ROWS, COLS), F32)


def call(kernel, name, ins, outs, shapes, scratch=(), us=1.0, mib=32, **more):
    return pl.pallas_call(
        kernel,
        in_specs=ins,
        out_specs=outs,
        out_shape=shapes,
        scratch_shapes=list(scratch),
        compiler_params=pltpu.CompilerParams(vmem_limit_bytes=mib * 2**20),
        cost_estimate=pl.CostEstimate(flops=int(us * 1e9), bytes_accessed=int(us * 2e6), transcendentals=0),
        name=name,
        **more,
    )


def pick_theirs(m, g, idx, weights):
    return call(
        theirs_kernel,
        "theirs",
        [HB] * 4,
        [VM] * 3,
        [
            jax.ShapeDtypeStruct((16, 128), F32),
            jax.ShapeDtypeStruct((32, 128), jnp.int32),
            DECODED,
        ],
        [
            pltpu.VMEM((LAYERS, ROWS, COLS), F32),
            pltpu.VMEM((LAYERS, ROWS, COLS), BF),
            pltpu.VMEM((BLOCKS, TOPK), jnp.int32),
            pltpu.VMEM((32, 128), jnp.int32),
            pltpu.VMEM(weights.shape, BF),
            pltpu.SemaphoreType.DMA((2 + 2 * LAYERS,)),
        ],
        2.5,
    )(m, g, idx, weights)


def pick_mine(acc, pos, weights):
    return call(mine_kernel, "mine", [VM] * 3, VM, jax.ShapeDtypeStruct((16, 128), F32), (), 1.7)(acc, pos, weights)


def own_update(which, acc, pos, v, cols, rows, out=None):
    ins, more = [acc, pos, v, cols, rows], {}
    if out is not None:
        ins.append(out)
        more = dict(input_output_aliases={5: 0})
    return call(
        lambda *refs: own_kernel(which, *refs),
        f"own{which}",
        [VM] * 5 + [HB] * (len(ins) - 5),
        HB,
        DECODED,
        [pltpu.VMEM((HALF, ROWS, COLS), F32), pltpu.SemaphoreType.DMA((HALF,))],
        2.2,
        **more,
    )(*ins)


def arrange(idx):
    shape = jax.ShapeDtypeStruct((BLOCKS // 2, 1024), F32)
    return call(arrange_kernel, "arrange", [VM], [VM, VM], [shape, shape], (), 0.5)(idx)


def add_sets(places, last, sets, fr, fc, old):
    ins, outs, shapes, more = [*(sets[s] for s in places), fr, fc], [VM], [GRIDS], {}
    first = old is None
    if not first:
        more = dict(input_output_aliases={len(ins): 0})
        ins.append(old)
    if last:
        outs.append(VM)
        shapes.append(jax.ShapeDtypeStruct((8, 128), F32))
    return call(
        lambda *refs: set_kernel(places, first, last, *refs),
        "sets" + "".join(str(s) for s in places),
        [VM] * len(ins),
        outs,
        shapes,
        [pltpu.VMEM((4, 16, 32 * SET * len(places)), F32)],
        1.4 * len(places),
        **more,
    )(*ins)


def decode(grid, cols, rows):
    return call(decode_kernel, "decode", [VM] * 3, VM, HALVED, (), 1.6)(grid, cols, rows)


def rescale(mine, theirs, total, out=None):
    ins, more = [mine, theirs, total], {}
    if out is not None:
        ins.append(out)
        more = dict(input_output_aliases={3: 0})
    return call(
        lambda *refs: scale_kernel(out is not None, *refs),
        "rescale" if out is None else "rescale_core0",
        [VM] * 3 + [HB] * (len(ins) - 3),
        HB,
        DECODED,
        [pltpu.VMEM((LAYERS, ROWS, COLS), F32), pltpu.VMEM((8, 128), F32), pltpu.SemaphoreType.DMA((LAYERS,))],
        1.4,
        **more,
    )(*ins)


def turn(x, axis, size, bit):
    return lax.ppermute(x, axis, [(i, i ^ bit) for i in range(size)])


def along_x(x, bit):
    pairs = [(p * 8 + t, p * 8 + (t ^ (bit if p & 1 else 1))) for p in range(REPLICAS) for t in range(8)]
    return lax.ppermute(x, ("dp", "tensor"), pairs)


def across(x):
    pairs = []
    for y in range(4):
        for z in range(8):
            for tx in range(4):
                to = (z + 6) % 8 if z in (0, 1, 4, 5) else (z + 2) % 8
                place = [((y * 4 + k % 4) * 2 + 1) * 8 + (k // 4) * 4 + tx for k in (z, to)]
                pairs.append(tuple(place))
                pairs.append((place[0] - 8, (place[0] - 8) ^ 1))
    return lax.ppermute(x, ("dp", "tensor"), pairs)


def on_device(momentum, gradient, kept_index):
    m, g = momentum[0], gradient[0]
    idx = kept_index.reshape(REPLICAS * BLOCKS, TOPK)
    forward, back_cols, back_rows = (jnp.asarray(x) for x in constants())
    held = [pltpu.with_memory_space_constraint(x, pltpu.HBM) for x in (m, g, idx, forward)]
    theirs, pos, acc = pick_theirs(*held)
    mine = pick_mine(acc, pos, forward)

    x = jnp.stack([mine, turn(theirs, "dp", REPLICAS, 1)])
    x, theirs, idx = lax.optimization_barrier((x, theirs, idx))
    x = jnp.concatenate([x] + [turn(x, "dp", REPLICAS, b) for b in (2, 4, 6)], axis=0)
    fr, fc = arrange(idx)
    momentum_out = own_update(0, acc, pos, theirs, back_cols, back_rows)
    x, momentum_out = lax.optimization_barrier((x, momentum_out))
    calls = ((0,), (1,), (3,), (2,))
    sets = {s: x if s == 0 else turn(x, "dp", REPLICAS, 8 * s) for c in calls for s in c}
    grid = None
    for places in calls[:-1]:
        (grid,) = add_sets(places, False, sets, fr, fc, grid)
    grid, squares = add_sets(calls[-1], True, sets, fr, fc, grid)

    total = squares + turn(squares, "dp", REPLICAS, 1)
    total, grid, mine = lax.optimization_barrier((total, grid, mine))
    other_grid = turn(grid, "dp", REPLICAS, 1)
    momentum_out = own_update(1, acc, pos, mine, back_cols, back_rows, momentum_out)
    decoded = decode(grid, back_cols, back_rows)
    total = total + along_x(total, 1)
    total, momentum_out, other_grid = lax.optimization_barrier((total, momentum_out, other_grid))
    other = decode(other_grid, back_cols, back_rows)
    total = total + along_x(total, 3)
    total, decoded, other = lax.optimization_barrier((total, decoded, other))
    total = total + across(total)
    given = turn(total, "dp", REPLICAS, 1)
    update = rescale(decoded, other, total)
    update = rescale(decoded, other, given, update)
    return (momentum_out[None], update)


def solution(mesh):
    placed = (
        P("dp", None, None, "tensor"),
        P("dp", None, None, "tensor"),
        P(None, None, None, "tensor", None),
    )
    return jax.shard_map(
        on_device,
        mesh=mesh,
        in_specs=placed,
        out_specs=(P("dp", None, None, "tensor"), P(None, None, "tensor")),
        check_vma=False,
    )
```

```python
import math

import jax
import jax.numpy as jnp
import ml_dtypes
import numpy as np
from jax import lax
from jax.experimental import pallas as pl
from jax.experimental.pallas import tpu as pltpu
from jax.sharding import PartitionSpec as P

GROUP = 64
TOPK = 32
REPLICAS = 32
LAYERS = 4
ROWS = 128
COLS = 1024
TILES = COLS // 256
BLOCKS = 128
SET = 8
ENTRIES = 128 * 8192
HALF = LAYERS // 2

decay_rate = 0.999
epsilon = 1e-06

BF = jnp.bfloat16
F32 = jnp.float32


def basis_matrix():
    f = np.arange(GROUP, dtype=np.float64)[:, None]
    n = np.arange(GROUP, dtype=np.float64)[None, :]
    scale = np.where(f == 0, math.sqrt(1.0 / GROUP), math.sqrt(2.0 / GROUP))
    return scale * np.cos(math.pi * (2.0 * n + 1.0) * f / (2.0 * GROUP))


def halves(x):
    x = x.astype(np.float32)
    hi = x.astype(ml_dtypes.bfloat16)
    lo = (x - hi.astype(np.float32)).astype(ml_dtypes.bfloat16)
    return hi, lo


def constants():
    w_hi, w_lo = halves(np.kron(np.eye(2), basis_matrix()))
    t_hi, t_lo = w_hi.T, w_lo.T
    none = np.zeros_like(w_lo)
    forward = np.block([[t_hi, t_lo], [t_hi, none]])
    back_cols = np.block([[w_hi, w_lo], [w_hi, none]])
    back_rows = np.block([[t_hi, t_hi], [t_lo, none]])
    return forward, back_cols, back_rows


def split(x):
    hi = x.astype(BF)
    return hi, (x - hi.astype(F32)).astype(BF)


def mm(a, b):
    return jnp.dot(a, b, preferred_element_type=F32)


def mm_t(a, b):
    return lax.dot_general(a, b, (((1,), (1,)), ((), ())), preferred_element_type=F32)


def times(x, weights):
    both = mm(jnp.concatenate(split(x), axis=1), weights)
    return both[:, :128] + both[:, 128:]


def lane_tiles(x):
    return jnp.concatenate([x[:, j : j + 128] for j in range(0, x.shape[1], 128)], axis=0)


def back(grids, cols, rows):
    half = times(jnp.concatenate([lane_tiles(x) for x in grids], axis=0), cols)
    out = []
    for t in range(TILES):
        part = half[t * 256 : t * 256 + 256]
        hi, lo = split(jnp.concatenate([part[:128], part[128:]], axis=1))
        both = mm(rows, jnp.concatenate([hi, lo], axis=0))
        out.append(both[:128] + both[128:])
    return out


def lane_block(shape):
    return lax.shift_right_logical(lax.broadcasted_iota(jnp.int32, shape, len(shape) - 1), 5) & 3


def columns(acc, weights):
    return times(lane_tiles(acc), weights)


def rows_and_pick(half, weights, pos_ref, row, v_ref, to):
    freq = lax.broadcasted_iota(jnp.int32, (GROUP, 128), 0)
    place = lax.broadcasted_iota(jnp.int32, (256, 256), 0)
    zeros = jnp.zeros((GROUP, 128), BF)
    for t in range(TILES):
        turned = [half[u * 128 : u * 128 + 128].T for u in (2 * t, 2 * t + 1)]
        hi, lo = split(times(jnp.concatenate(turned, axis=0), weights))
        pos = [pos_ref[pl.ds(row + a * 4 + t, 1), :] for a in range(2)]
        hot = [(freq == lax.shift_right_logical(x, 6)).astype(F32).astype(BF) for x in pos]
        pick = jnp.concatenate(
            [
                jnp.concatenate([hot[0], zeros], axis=1),
                jnp.concatenate([zeros, hot[1]], axis=1),
            ],
            axis=0,
        )
        got = mm(jnp.concatenate([hi, lo], axis=1), jnp.concatenate([pick, pick], axis=0))
        where = jnp.concatenate([(x & 63) + 64 * lane_block((1, 128)) for x in pos], axis=1)
        v = jnp.sum(jnp.where(place == where, got, 0.0), axis=0, keepdims=True)
        for a in range(2):
            v_ref[pl.ds(to + a * 4 + t, 1), :] = v[:, a * 128 : a * 128 + 128]


def theirs_kernel(m_hbm, g_hbm, idx_hbm, weights_hbm, v_ref, pos_ref, acc_ref, m_buf, g_buf, idx_buf, all_ref, weights_ref, sems):
    p = lax.axis_index("dp")
    core = p & 1
    order = [HALF - HALF * core + i for i in range(HALF)] + [HALF * core + i for i in range(HALF)]
    small = [
        pltpu.make_async_copy(weights_hbm, weights_ref, sems.at[0]),
        pltpu.make_async_copy(idx_hbm.at[pl.ds(p * BLOCKS, BLOCKS)], idx_buf, sems.at[1]),
    ]
    large = [
        (
            pltpu.make_async_copy(m_hbm.at[l], m_buf.at[i], sems.at[2 + 2 * i]),
            pltpu.make_async_copy(g_hbm.at[l], g_buf.at[i], sems.at[3 + 2 * i]),
        )
        for i, l in enumerate(order)
    ]
    for copy in (*large[0], *small, *large[1], *large[2], *large[3]):
        copy.start()

    def accumulate(i):
        acc = decay_rate * m_buf[i] + g_buf[i].astype(F32)
        acc_ref[i] = acc
        return acc

    def wait(i):
        for copy in large[i]:
            copy.wait()

    wait(0)
    for copy in small:
        copy.wait()
    all_ref[...] = jnp.concatenate([idx_buf[pl.ds(cj, 32, stride=4), :] for cj in range(4)], axis=1)
    pos_ref[:16] = all_ref[pl.ds(pl.multiple_of(16 - core * 16, 16), 16), :]
    pos_ref[16:] = all_ref[pl.ds(pl.multiple_of(core * 16, 16), 16), :]
    rows_and_pick(columns(accumulate(0), weights_ref[...]), weights_ref[...], pos_ref, 0, v_ref, 0)
    for i in range(1, LAYERS):
        wait(i)
    rows_and_pick(columns(accumulate(1), weights_ref[...]), weights_ref[...], pos_ref, 8, v_ref, 8)
    for i in range(HALF, LAYERS):
        accumulate(i)


def mine_kernel(acc_ref, pos_ref, weights_ref, v_ref):
    halves_of = [columns(acc_ref[HALF + i], weights_ref[...]) for i in range(HALF)]
    for i in range(HALF):
        rows_and_pick(halves_of[i], weights_ref[...], pos_ref, 16 + 8 * i, v_ref, 8 * i)


def own_kernel(which, acc_ref, own_ref, v_ref, cols_ref, rows_ref, *rest):
    out_hbm, out_buf, sems = rest[-3:]
    freq = lax.broadcasted_iota(jnp.int32, (GROUP, 128), 0)
    place = lax.broadcasted_iota(jnp.int32, (256, 128), 0)
    zeros = jnp.zeros((GROUP, 128), BF)
    copies = []
    core = lax.axis_index("dp") & 1
    start = HALF - HALF * core if which == 0 else HALF * core
    for i in range(HALF):
        l = which * HALF + i
        grids = []
        for t in range(TILES):
            left, right = [], []
            for a in range(2):
                row = l * 8 + a * 4 + t
                pos = own_ref[pl.ds(row, 1), :]
                v = v_ref[pl.ds(i * 8 + a * 4 + t, 1), :]
                left.append(split(jnp.where(freq == lax.shift_right_logical(pos, 6), v, 0.0)))
                right.append((place == (pos & 63) + 64 * lane_block((1, 128))).astype(F32).astype(BF))
            rows = []
            for h in range(2):
                rows.append(jnp.concatenate([left[0][h], zeros], axis=1))
                rows.append(jnp.concatenate([zeros, left[1][h]], axis=1))
            both = mm_t(jnp.concatenate(rows, axis=0), jnp.concatenate(right, axis=1))
            grids.append(both[:128] + both[128:])
        for t, tile in enumerate(back(grids, cols_ref[...], rows_ref[...])):
            s = slice(t * 256, t * 256 + 256)
            out_buf[i, :, s] = acc_ref[l, :, s] - tile
        copies.append(pltpu.make_async_copy(out_buf.at[i], out_hbm.at[start + i], sems.at[i]))
        copies[-1].start()
    for copy in copies:
        copy.wait()


def arrange_kernel(idx_ref, fr_ref, fc_ref):
    p = lax.axis_index("dp")
    half = BLOCKS // 2
    start = (p & 1) * half
    for q in range(REPLICAS // 4):
        pos = jnp.concatenate([idx_ref[pl.ds(pl.multiple_of((p ^ (4 * q + j)) * BLOCKS + start, half), half), :] for j in range(4)], axis=1)
        fr_ref[:, q * 128 : q * 128 + 128] = lax.shift_right_logical(pos, 6).astype(F32)
        fc_ref[:, q * 128 : q * 128 + 128] = (pos & 63).astype(F32)


def set_kernel(places, first, last, *rest):
    v_refs, (fr_ref, fc_ref), rest = rest[: len(places)], rest[len(places) : len(places) + 2], rest[len(places) + 2 :]
    old_ref = None
    if not first:
        old_ref, rest = rest[0], rest[1:]
    if last:
        grid_ref, sq_ref, val_ref = rest
        first_layer = (lax.axis_index("dp") & 1) * HALF
        sq_ref[...] = jnp.zeros_like(sq_ref)
    else:
        grid_ref, val_ref = rest
    lane = lane_block((16, 128))
    for n, v_ref in enumerate(v_refs):
        for q in range(SET // 4):
            x = [v_ref[4 * q + j] for j in range(4)]
            for cj in range(4):
                y = jnp.zeros((16, 128), F32)
                for j in range(4):
                    moved = x[j] if j == cj else pltpu.roll(x[j], ((j - cj) * 32) % 128, 1)
                    y = jnp.where(lane == j, moved, y)
                start = (n * SET // 4 + q) * 128
                val_ref[cj, :, start : start + 128] = y
    wide = 32 * SET
    freq = lax.broadcasted_iota(jnp.int32, (GROUP, wide), 0).astype(F32).astype(BF)
    zero, one = jnp.zeros((), BF), jnp.ones((), BF)
    for l in range(HALF):
        squares = jnp.zeros((1, 256), F32)
        for i in range(2 * TILES):
            a, t = i // TILES, i % TILES
            parts = []
            for cj in range(4):
                row = l * 32 + i * 4 + cj
                left, right = [], []
                for n, place in enumerate(places):
                    s = slice(place * wide, place * wide + wide)
                    fr = fr_ref[pl.ds(row, 1), s].astype(BF)
                    fc = fc_ref[pl.ds(row, 1), s].astype(BF)
                    hi, lo = split(val_ref[cj, pl.ds(l * 8 + i, 1), n * wide : n * wide + wide])
                    at = freq == fr
                    left.append(jnp.concatenate([jnp.where(at, hi, zero), jnp.where(at, lo, zero)], axis=0))
                    right.append(jnp.where(freq == fc, one, zero))
                both = mm_t(jnp.concatenate(left, axis=1), jnp.concatenate(right, axis=1))
                parts.append(both[:GROUP] + both[GROUP:])
            grid = jnp.concatenate(parts, axis=1)
            if old_ref is not None:
                grid = grid + old_ref[l, t, a * GROUP : a * GROUP + GROUP, :]
            grid_ref[l, t, a * GROUP : a * GROUP + GROUP, :] = grid
            if last:
                squares = squares + jnp.sum(grid * grid, axis=0, keepdims=True)
        if last:
            sq_ref[pl.ds(first_layer + l, 1), :] = squares[:, :128] + squares[:, 128:]


def decode_kernel(grid_ref, cols_ref, rows_ref, out_ref):
    def body(l, carry):
        tiles = back([grid_ref[l, t] for t in range(TILES)], cols_ref[...], rows_ref[...])
        for t, tile in enumerate(tiles):
            out_ref[l, :, t * 256 : t * 256 + 256] = tile
        return carry

    for l in range(HALF):
        body(l, 0)


def scale_kernel(again, mine_ref, theirs_ref, total_ref, *rest):
    out_hbm, out_buf, factor_ref, sems = rest[-4:]
    core = lax.axis_index("dp") & 1

    def scale():
        total = jnp.sum(total_ref[...], axis=1, keepdims=True)
        factor_ref[...] = lax.rsqrt(jnp.broadcast_to(total, (8, 128)) / ENTRIES + epsilon)
        copies = []
        for ref, start in ((mine_ref, core * HALF), (theirs_ref, HALF - core * HALF)):
            for i in range(HALF):
                l = start + i
                row = factor_ref[pl.ds(l, 1), :]
                for t in range(COLS // 128):
                    s = slice(t * 128, t * 128 + 128)
                    out_buf[l, :, s] = ref[i, :, s] * row
                copies.append(pltpu.make_async_copy(out_buf.at[l], out_hbm.at[l], sems.at[len(copies)]))
                copies[-1].start()
        for copy in copies:
            copy.wait()

    if again:
        pl.when(core == 0)(scale)
    else:
        scale()


VM = pl.BlockSpec(memory_space=pltpu.VMEM)
HB = pl.BlockSpec(memory_space=pltpu.HBM)
DECODED = jax.ShapeDtypeStruct((LAYERS, ROWS, COLS), F32)
GRIDS = jax.ShapeDtypeStruct((HALF, TILES, 128, 256), F32)
HALVED = jax.ShapeDtypeStruct((HALF, ROWS, COLS), F32)


def call(kernel, name, ins, outs, shapes, scratch=(), us=1.0, mib=32, **more):
    return pl.pallas_call(
        kernel,
        in_specs=ins,
        out_specs=outs,
        out_shape=shapes,
        scratch_shapes=list(scratch),
        compiler_params=pltpu.CompilerParams(vmem_limit_bytes=mib * 2**20),
        cost_estimate=pl.CostEstimate(flops=int(us * 1e9), bytes_accessed=int(us * 2e6), transcendentals=0),
        name=name,
        **more,
    )


def pick_theirs(m, g, idx, weights):
    return call(
        theirs_kernel,
        "theirs",
        [HB] * 4,
        [VM] * 3,
        [
            jax.ShapeDtypeStruct((16, 128), F32),
            jax.ShapeDtypeStruct((32, 128), jnp.int32),
            DECODED,
        ],
        [
            pltpu.VMEM((LAYERS, ROWS, COLS), F32),
            pltpu.VMEM((LAYERS, ROWS, COLS), BF),
            pltpu.VMEM((BLOCKS, TOPK), jnp.int32),
            pltpu.VMEM((32, 128), jnp.int32),
            pltpu.VMEM(weights.shape, BF),
            pltpu.SemaphoreType.DMA((2 + 2 * LAYERS,)),
        ],
        2.5,
    )(m, g, idx, weights)


def pick_mine(acc, pos, weights):
    return call(mine_kernel, "mine", [VM] * 3, VM, jax.ShapeDtypeStruct((16, 128), F32), (), 1.7)(acc, pos, weights)


def own_update(which, acc, pos, v, cols, rows, out=None):
    ins, more = [acc, pos, v, cols, rows], {}
    if out is not None:
        ins.append(out)
        more = dict(input_output_aliases={5: 0})
    return call(
        lambda *refs: own_kernel(which, *refs),
        f"own{which}",
        [VM] * 5 + [HB] * (len(ins) - 5),
        HB,
        DECODED,
        [pltpu.VMEM((HALF, ROWS, COLS), F32), pltpu.SemaphoreType.DMA((HALF,))],
        2.2,
        **more,
    )(*ins)


def arrange(idx):
    shape = jax.ShapeDtypeStruct((BLOCKS // 2, 1024), F32)
    return call(arrange_kernel, "arrange", [VM], [VM, VM], [shape, shape], (), 0.5)(idx)


def add_sets(places, last, sets, fr, fc, old):
    ins, outs, shapes, more = [*(sets[s] for s in places), fr, fc], [VM], [GRIDS], {}
    first = old is None
    if not first:
        more = dict(input_output_aliases={len(ins): 0})
        ins.append(old)
    if last:
        outs.append(VM)
        shapes.append(jax.ShapeDtypeStruct((8, 128), F32))
    return call(
        lambda *refs: set_kernel(places, first, last, *refs),
        "sets" + "".join(str(s) for s in places),
        [VM] * len(ins),
        outs,
        shapes,
        [pltpu.VMEM((4, 16, 32 * SET * len(places)), F32)],
        1.4 * len(places),
        **more,
    )(*ins)


def decode(grid, cols, rows):
    return call(decode_kernel, "decode", [VM] * 3, VM, HALVED, (), 1.6)(grid, cols, rows)


def rescale(mine, theirs, total, out=None):
    ins, more = [mine, theirs, total], {}
    if out is not None:
        ins.append(out)
        more = dict(input_output_aliases={3: 0})
    return call(
        lambda *refs: scale_kernel(out is not None, *refs),
        "rescale" if out is None else "rescale_core0",
        [VM] * 3 + [HB] * (len(ins) - 3),
        HB,
        DECODED,
        [pltpu.VMEM((LAYERS, ROWS, COLS), F32), pltpu.VMEM((8, 128), F32), pltpu.SemaphoreType.DMA((LAYERS,))],
        1.4,
        **more,
    )(*ins)


def turn(x, axis, size, bit):
    return lax.ppermute(x, axis, [(i, i ^ bit) for i in range(size)])


def along_x(x, bit):
    pairs = [(p * 8 + t, p * 8 + (t ^ (bit if p & 1 else 1))) for p in range(REPLICAS) for t in range(8)]
    return lax.ppermute(x, ("dp", "tensor"), pairs)


def across(x):
    pairs = []
    for y in range(4):
        for z in range(8):
            for tx in range(4):
                to = (z + 6) % 8 if z in (0, 1, 4, 5) else (z + 2) % 8
                place = [((y * 4 + k % 4) * 2 + 1) * 8 + (k // 4) * 4 + tx for k in (z, to)]
                pairs.append(tuple(place))
                pairs.append((place[0] - 8, (place[0] - 8) ^ 1))
    return lax.ppermute(x, ("dp", "tensor"), pairs)


def on_device(momentum, gradient, kept_index):
    m, g = momentum[0], gradient[0]
    idx = kept_index.reshape(REPLICAS * BLOCKS, TOPK)
    forward, back_cols, back_rows = (jnp.asarray(x) for x in constants())
    held = [pltpu.with_memory_space_constraint(x, pltpu.HBM) for x in (m, g, idx, forward)]
    theirs, pos, acc = pick_theirs(*held)
    mine = pick_mine(acc, pos, forward)

    x = jnp.stack([mine, turn(theirs, "dp", REPLICAS, 1)])
    x, theirs, idx = lax.optimization_barrier((x, theirs, idx))
    x = jnp.concatenate([x] + [turn(x, "dp", REPLICAS, b) for b in (2, 4, 6)], axis=0)
    fr, fc = arrange(idx)
    momentum_out = own_update(0, acc, pos, theirs, back_cols, back_rows)
    x, momentum_out = lax.optimization_barrier((x, momentum_out))
    calls = ((0,), (1,), (3,), (2,))
    sets = {s: x if s == 0 else turn(x, "dp", REPLICAS, 8 * s) for c in calls for s in c}
    grid = None
    for places in calls[:-1]:
        (grid,) = add_sets(places, False, sets, fr, fc, grid)
    grid, squares = add_sets(calls[-1], True, sets, fr, fc, grid)

    total = squares + turn(squares, "dp", REPLICAS, 1)
    total, grid, mine = lax.optimization_barrier((total, grid, mine))
    other_grid = turn(grid, "dp", REPLICAS, 1)
    momentum_out = own_update(1, acc, pos, mine, back_cols, back_rows, momentum_out)
    total = total + along_x(total, 1)
    total, momentum_out, grid, other_grid = lax.optimization_barrier((total, momentum_out, grid, other_grid))
    decoded = decode(grid, back_cols, back_rows)
    other = decode(other_grid, back_cols, back_rows)
    total = total + along_x(total, 3)
    total, decoded, other = lax.optimization_barrier((total, decoded, other))
    total = total + across(total)
    given = turn(total, "dp", REPLICAS, 1)
    update = rescale(decoded, other, total)
    update = rescale(decoded, other, given, update)
    return (momentum_out[None], update)


def solution(mesh):
    placed = (
        P("dp", None, None, "tensor"),
        P("dp", None, None, "tensor"),
        P(None, None, None, "tensor", None),
    )
    return jax.shard_map(
        on_device,
        mesh=mesh,
        in_specs=placed,
        out_specs=(P("dp", None, None, "tensor"), P(None, None, "tensor")),
        check_vma=False,
    )
```

```python
import math

import jax
import jax.numpy as jnp
import ml_dtypes
import numpy as np
from jax import lax
from jax.experimental import pallas as pl
from jax.experimental.pallas import tpu as pltpu
from jax.sharding import PartitionSpec as P

GROUP = 64
TOPK = 32
REPLICAS = 32
LAYERS = 4
ROWS = 128
COLS = 1024
TILES = COLS // 256
BLOCKS = 128
SET = 8
ENTRIES = 128 * 8192
HALF = LAYERS // 2

decay_rate = 0.999
epsilon = 1e-06

BF = jnp.bfloat16
F32 = jnp.float32


def basis_matrix():
    f = np.arange(GROUP, dtype=np.float64)[:, None]
    n = np.arange(GROUP, dtype=np.float64)[None, :]
    scale = np.where(f == 0, math.sqrt(1.0 / GROUP), math.sqrt(2.0 / GROUP))
    return scale * np.cos(math.pi * (2.0 * n + 1.0) * f / (2.0 * GROUP))


def halves(x):
    x = x.astype(np.float32)
    hi = x.astype(ml_dtypes.bfloat16)
    lo = (x - hi.astype(np.float32)).astype(ml_dtypes.bfloat16)
    return hi, lo


def constants():
    w_hi, w_lo = halves(np.kron(np.eye(2), basis_matrix()))
    t_hi, t_lo = w_hi.T, w_lo.T
    none = np.zeros_like(w_lo)
    forward = np.block([[t_hi, t_lo], [t_hi, none]])
    back_cols = np.block([[w_hi, w_lo], [w_hi, none]])
    back_rows = np.block([[t_hi, t_hi], [t_lo, none]])
    return forward, back_cols, back_rows


def split(x):
    hi = x.astype(BF)
    return hi, (x - hi.astype(F32)).astype(BF)


def mm(a, b):
    return jnp.dot(a, b, preferred_element_type=F32)


def mm_t(a, b):
    return lax.dot_general(a, b, (((1,), (1,)), ((), ())), preferred_element_type=F32)


def times(x, weights):
    both = mm(jnp.concatenate(split(x), axis=1), weights)
    return both[:, :128] + both[:, 128:]


def lane_tiles(x):
    return jnp.concatenate([x[:, j : j + 128] for j in range(0, x.shape[1], 128)], axis=0)


def back(grids, cols, rows):
    half = times(jnp.concatenate([lane_tiles(x) for x in grids], axis=0), cols)
    out = []
    for t in range(TILES):
        part = half[t * 256 : t * 256 + 256]
        hi, lo = split(jnp.concatenate([part[:128], part[128:]], axis=1))
        both = mm(rows, jnp.concatenate([hi, lo], axis=0))
        out.append(both[:128] + both[128:])
    return out


def lane_block(shape):
    return lax.shift_right_logical(lax.broadcasted_iota(jnp.int32, shape, len(shape) - 1), 5) & 3


def columns(acc, weights):
    return times(lane_tiles(acc), weights)


def rows_and_pick(half, weights, pos_ref, row, v_ref, to):
    freq = lax.broadcasted_iota(jnp.int32, (GROUP, 128), 0)
    place = lax.broadcasted_iota(jnp.int32, (256, 256), 0)
    zeros = jnp.zeros((GROUP, 128), BF)
    for t in range(TILES):
        turned = [half[u * 128 : u * 128 + 128].T for u in (2 * t, 2 * t + 1)]
        hi, lo = split(times(jnp.concatenate(turned, axis=0), weights))
        pos = [pos_ref[pl.ds(row + a * 4 + t, 1), :] for a in range(2)]
        hot = [(freq == lax.shift_right_logical(x, 6)).astype(F32).astype(BF) for x in pos]
        pick = jnp.concatenate(
            [
                jnp.concatenate([hot[0], zeros], axis=1),
                jnp.concatenate([zeros, hot[1]], axis=1),
            ],
            axis=0,
        )
        got = mm(jnp.concatenate([hi, lo], axis=1), jnp.concatenate([pick, pick], axis=0))
        where = jnp.concatenate([(x & 63) + 64 * lane_block((1, 128)) for x in pos], axis=1)
        v = jnp.sum(jnp.where(place == where, got, 0.0), axis=0, keepdims=True)
        for a in range(2):
            v_ref[pl.ds(to + a * 4 + t, 1), :] = v[:, a * 128 : a * 128 + 128]


def theirs_kernel(m_hbm, g_hbm, idx_hbm, weights_hbm, v_ref, pos_ref, acc_ref, m_buf, g_buf, idx_buf, all_ref, weights_ref, sems):
    p = lax.axis_index("dp")
    core = p & 1
    order = [HALF - HALF * core + i for i in range(HALF)] + [HALF * core + i for i in range(HALF)]
    small = [
        pltpu.make_async_copy(weights_hbm, weights_ref, sems.at[0]),
        pltpu.make_async_copy(idx_hbm.at[pl.ds(p * BLOCKS, BLOCKS)], idx_buf, sems.at[1]),
    ]
    large = [
        (
            pltpu.make_async_copy(m_hbm.at[l], m_buf.at[i], sems.at[2 + 2 * i]),
            pltpu.make_async_copy(g_hbm.at[l], g_buf.at[i], sems.at[3 + 2 * i]),
        )
        for i, l in enumerate(order)
    ]
    for copy in (*large[0], *small, *large[1], *large[2], *large[3]):
        copy.start()

    def accumulate(i):
        acc = decay_rate * m_buf[i] + g_buf[i].astype(F32)
        acc_ref[i] = acc
        return acc

    def wait(i):
        for copy in large[i]:
            copy.wait()

    wait(0)
    for copy in small:
        copy.wait()
    all_ref[...] = jnp.concatenate([idx_buf[pl.ds(cj, 32, stride=4), :] for cj in range(4)], axis=1)
    pos_ref[:16] = all_ref[pl.ds(pl.multiple_of(16 - core * 16, 16), 16), :]
    pos_ref[16:] = all_ref[pl.ds(pl.multiple_of(core * 16, 16), 16), :]
    rows_and_pick(columns(accumulate(0), weights_ref[...]), weights_ref[...], pos_ref, 0, v_ref, 0)
    for i in range(1, LAYERS):
        wait(i)
    rows_and_pick(columns(accumulate(1), weights_ref[...]), weights_ref[...], pos_ref, 8, v_ref, 8)
    for i in range(HALF, LAYERS):
        accumulate(i)


def mine_kernel(acc_ref, pos_ref, weights_ref, v_ref):
    halves_of = [columns(acc_ref[HALF + i], weights_ref[...]) for i in range(HALF)]
    for i in range(HALF):
        rows_and_pick(halves_of[i], weights_ref[...], pos_ref, 16 + 8 * i, v_ref, 8 * i)


def own_kernel(which, acc_ref, own_ref, v_ref, cols_ref, rows_ref, *rest):
    out_hbm, out_buf, sems = rest[-3:]
    freq = lax.broadcasted_iota(jnp.int32, (GROUP, 128), 0)
    place = lax.broadcasted_iota(jnp.int32, (256, 128), 0)
    zeros = jnp.zeros((GROUP, 128), BF)
    copies = []
    core = lax.axis_index("dp") & 1
    start = HALF - HALF * core if which == 0 else HALF * core
    for i in range(HALF):
        l = which * HALF + i
        grids = []
        for t in range(TILES):
            left, right = [], []
            for a in range(2):
                row = l * 8 + a * 4 + t
                pos = own_ref[pl.ds(row, 1), :]
                v = v_ref[pl.ds(i * 8 + a * 4 + t, 1), :]
                left.append(split(jnp.where(freq == lax.shift_right_logical(pos, 6), v, 0.0)))
                right.append((place == (pos & 63) + 64 * lane_block((1, 128))).astype(F32).astype(BF))
            rows = []
            for h in range(2):
                rows.append(jnp.concatenate([left[0][h], zeros], axis=1))
                rows.append(jnp.concatenate([zeros, left[1][h]], axis=1))
            both = mm_t(jnp.concatenate(rows, axis=0), jnp.concatenate(right, axis=1))
            grids.append(both[:128] + both[128:])
        for t, tile in enumerate(back(grids, cols_ref[...], rows_ref[...])):
            s = slice(t * 256, t * 256 + 256)
            out_buf[i, :, s] = acc_ref[l, :, s] - tile
        copies.append(pltpu.make_async_copy(out_buf.at[i], out_hbm.at[start + i], sems.at[i]))
        copies[-1].start()
    for copy in copies:
        copy.wait()


def arrange_kernel(idx_ref, fr_ref, fc_ref):
    p = lax.axis_index("dp")
    half = BLOCKS // 2
    start = (p & 1) * half
    for q in range(REPLICAS // 4):
        pos = jnp.concatenate([idx_ref[pl.ds(pl.multiple_of((p ^ (4 * q + j)) * BLOCKS + start, half), half), :] for j in range(4)], axis=1)
        fr_ref[:, q * 128 : q * 128 + 128] = lax.shift_right_logical(pos, 6).astype(F32)
        fc_ref[:, q * 128 : q * 128 + 128] = (pos & 63).astype(F32)


def set_kernel(places, first, last, *rest):
    v_refs, (fr_ref, fc_ref), rest = rest[: len(places)], rest[len(places) : len(places) + 2], rest[len(places) + 2 :]
    old_ref = None
    if not first:
        old_ref, rest = rest[0], rest[1:]
    if last:
        grid_ref, sq_ref, val_ref = rest
        first_layer = (lax.axis_index("dp") & 1) * HALF
        sq_ref[...] = jnp.zeros_like(sq_ref)
    else:
        grid_ref, val_ref = rest
    lane = lane_block((16, 128))
    for n, v_ref in enumerate(v_refs):
        for q in range(SET // 4):
            x = [v_ref[4 * q + j] for j in range(4)]
            for cj in range(4):
                y = jnp.zeros((16, 128), F32)
                for j in range(4):
                    moved = x[j] if j == cj else pltpu.roll(x[j], ((j - cj) * 32) % 128, 1)
                    y = jnp.where(lane == j, moved, y)
                start = (n * SET // 4 + q) * 128
                val_ref[cj, :, start : start + 128] = y
    wide = 32 * SET
    freq = lax.broadcasted_iota(jnp.int32, (GROUP, wide), 0).astype(F32).astype(BF)
    zero, one = jnp.zeros((), BF), jnp.ones((), BF)
    for l in range(HALF):
        squares = jnp.zeros((1, 256), F32)
        for i in range(2 * TILES):
            a, t = i // TILES, i % TILES
            parts = []
            for cj in range(4):
                row = l * 32 + i * 4 + cj
                left, right = [], []
                for n, place in enumerate(places):
                    s = slice(place * wide, place * wide + wide)
                    fr = fr_ref[pl.ds(row, 1), s].astype(BF)
                    fc = fc_ref[pl.ds(row, 1), s].astype(BF)
                    hi, lo = split(val_ref[cj, pl.ds(l * 8 + i, 1), n * wide : n * wide + wide])
                    at = freq == fr
                    left.append(jnp.concatenate([jnp.where(at, hi, zero), jnp.where(at, lo, zero)], axis=0))
                    right.append(jnp.where(freq == fc, one, zero))
                both = mm_t(jnp.concatenate(left, axis=1), jnp.concatenate(right, axis=1))
                parts.append(both[:GROUP] + both[GROUP:])
            grid = jnp.concatenate(parts, axis=1)
            if old_ref is not None:
                grid = grid + old_ref[l, t, a * GROUP : a * GROUP + GROUP, :]
            grid_ref[l, t, a * GROUP : a * GROUP + GROUP, :] = grid
            if last:
                squares = squares + jnp.sum(grid * grid, axis=0, keepdims=True)
        if last:
            sq_ref[pl.ds(first_layer + l, 1), :] = squares[:, :128] + squares[:, 128:]


def decode_kernel(grid_ref, cols_ref, rows_ref, out_ref):
    def body(l, carry):
        tiles = back([grid_ref[l, t] for t in range(TILES)], cols_ref[...], rows_ref[...])
        for t, tile in enumerate(tiles):
            out_ref[l, :, t * 256 : t * 256 + 256] = tile
        return carry

    for l in range(HALF):
        body(l, 0)


def scale_kernel(again, mine_ref, theirs_ref, total_ref, *rest):
    out_hbm, out_buf, factor_ref, sems = rest[-4:]
    core = lax.axis_index("dp") & 1

    def scale():
        total = jnp.sum(total_ref[...], axis=1, keepdims=True)
        factor_ref[...] = lax.rsqrt(jnp.broadcast_to(total, (8, 128)) / ENTRIES + epsilon)
        copies = []
        for ref, start in ((mine_ref, core * HALF), (theirs_ref, HALF - core * HALF)):
            for i in range(HALF):
                l = start + i
                row = factor_ref[pl.ds(l, 1), :]
                for t in range(COLS // 128):
                    s = slice(t * 128, t * 128 + 128)
                    out_buf[l, :, s] = ref[i, :, s] * row
                copies.append(pltpu.make_async_copy(out_buf.at[l], out_hbm.at[l], sems.at[len(copies)]))
                copies[-1].start()
        for copy in copies:
            copy.wait()

    pl.when(core == (0 if again else 1))(scale)


VM = pl.BlockSpec(memory_space=pltpu.VMEM)
HB = pl.BlockSpec(memory_space=pltpu.HBM)
DECODED = jax.ShapeDtypeStruct((LAYERS, ROWS, COLS), F32)
GRIDS = jax.ShapeDtypeStruct((HALF, TILES, 128, 256), F32)
HALVED = jax.ShapeDtypeStruct((HALF, ROWS, COLS), F32)


def call(kernel, name, ins, outs, shapes, scratch=(), us=1.0, mib=32, **more):
    return pl.pallas_call(
        kernel,
        in_specs=ins,
        out_specs=outs,
        out_shape=shapes,
        scratch_shapes=list(scratch),
        compiler_params=pltpu.CompilerParams(vmem_limit_bytes=mib * 2**20),
        cost_estimate=pl.CostEstimate(flops=int(us * 1e9), bytes_accessed=int(us * 2e6), transcendentals=0),
        name=name,
        **more,
    )


def pick_theirs(m, g, idx, weights):
    return call(
        theirs_kernel,
        "theirs",
        [HB] * 4,
        [VM] * 3,
        [
            jax.ShapeDtypeStruct((16, 128), F32),
            jax.ShapeDtypeStruct((32, 128), jnp.int32),
            DECODED,
        ],
        [
            pltpu.VMEM((LAYERS, ROWS, COLS), F32),
            pltpu.VMEM((LAYERS, ROWS, COLS), BF),
            pltpu.VMEM((BLOCKS, TOPK), jnp.int32),
            pltpu.VMEM((32, 128), jnp.int32),
            pltpu.VMEM(weights.shape, BF),
            pltpu.SemaphoreType.DMA((2 + 2 * LAYERS,)),
        ],
        2.5,
    )(m, g, idx, weights)


def pick_mine(acc, pos, weights):
    return call(mine_kernel, "mine", [VM] * 3, VM, jax.ShapeDtypeStruct((16, 128), F32), (), 1.7)(acc, pos, weights)


def own_update(which, acc, pos, v, cols, rows, out=None):
    ins, more = [acc, pos, v, cols, rows], {}
    if out is not None:
        ins.append(out)
        more = dict(input_output_aliases={5: 0})
    return call(
        lambda *refs: own_kernel(which, *refs),
        f"own{which}",
        [VM] * 5 + [HB] * (len(ins) - 5),
        HB,
        DECODED,
        [pltpu.VMEM((HALF, ROWS, COLS), F32), pltpu.SemaphoreType.DMA((HALF,))],
        2.2,
        **more,
    )(*ins)


def arrange(idx):
    shape = jax.ShapeDtypeStruct((BLOCKS // 2, 1024), F32)
    return call(arrange_kernel, "arrange", [VM], [VM, VM], [shape, shape], (), 0.5)(idx)


def add_sets(places, last, sets, fr, fc, old):
    ins, outs, shapes, more = [*(sets[s] for s in places), fr, fc], [VM], [GRIDS], {}
    first = old is None
    if not first:
        more = dict(input_output_aliases={len(ins): 0})
        ins.append(old)
    if last:
        outs.append(VM)
        shapes.append(jax.ShapeDtypeStruct((8, 128), F32))
    return call(
        lambda *refs: set_kernel(places, first, last, *refs),
        "sets" + "".join(str(s) for s in places),
        [VM] * len(ins),
        outs,
        shapes,
        [pltpu.VMEM((4, 16, 32 * SET * len(places)), F32)],
        1.4 * len(places),
        **more,
    )(*ins)


def decode(grid, cols, rows):
    return call(decode_kernel, "decode", [VM] * 3, VM, HALVED, (), 1.6)(grid, cols, rows)


def rescale(mine, theirs, total, out=None):
    ins, more = [mine, theirs, total], {}
    if out is not None:
        ins.append(out)
        more = dict(input_output_aliases={3: 0})
    return call(
        lambda *refs: scale_kernel(out is not None, *refs),
        "rescale" if out is None else "rescale_core0",
        [VM] * 3 + [HB] * (len(ins) - 3),
        HB,
        DECODED,
        [pltpu.VMEM((LAYERS, ROWS, COLS), F32), pltpu.VMEM((8, 128), F32), pltpu.SemaphoreType.DMA((LAYERS,))],
        1.4,
        **more,
    )(*ins)


def turn(x, axis, size, bit):
    return lax.ppermute(x, axis, [(i, i ^ bit) for i in range(size)])


def along_x(x, bit):
    pairs = [(p * 8 + t, p * 8 + (t ^ (bit if p & 1 else 1))) for p in range(REPLICAS) for t in range(8)]
    return lax.ppermute(x, ("dp", "tensor"), pairs)


def across(x):
    pairs = []
    for y in range(4):
        for z in range(8):
            for tx in range(4):
                to = (z + 6) % 8 if z in (0, 1, 4, 5) else (z + 2) % 8
                place = [((y * 4 + k % 4) * 2 + 1) * 8 + (k // 4) * 4 + tx for k in (z, to)]
                pairs.append(tuple(place))
                pairs.append((place[0] - 8, (place[0] - 8) ^ 1))
    return lax.ppermute(x, ("dp", "tensor"), pairs)


def on_device(momentum, gradient, kept_index):
    m, g = momentum[0], gradient[0]
    idx = kept_index.reshape(REPLICAS * BLOCKS, TOPK)
    forward, back_cols, back_rows = (jnp.asarray(x) for x in constants())
    held = [pltpu.with_memory_space_constraint(x, pltpu.HBM) for x in (m, g, idx, forward)]
    theirs, pos, acc = pick_theirs(*held)
    mine = pick_mine(acc, pos, forward)

    x = jnp.stack([mine, turn(theirs, "dp", REPLICAS, 1)])
    x, theirs, idx = lax.optimization_barrier((x, theirs, idx))
    x = jnp.concatenate([x] + [turn(x, "dp", REPLICAS, b) for b in (2, 4, 6)], axis=0)
    fr, fc = arrange(idx)
    momentum_out = own_update(0, acc, pos, theirs, back_cols, back_rows)
    x, momentum_out = lax.optimization_barrier((x, momentum_out))
    calls = ((0,), (1,), (3,), (2,))
    sets = {s: x if s == 0 else turn(x, "dp", REPLICAS, 8 * s) for c in calls for s in c}
    grid = None
    for places in calls[:-1]:
        (grid,) = add_sets(places, False, sets, fr, fc, grid)
    grid, squares = add_sets(calls[-1], True, sets, fr, fc, grid)

    total = squares + turn(squares, "dp", REPLICAS, 1)
    total, grid, mine = lax.optimization_barrier((total, grid, mine))
    other_grid = turn(grid, "dp", REPLICAS, 1)
    momentum_out = own_update(1, acc, pos, mine, back_cols, back_rows, momentum_out)
    total = total + along_x(total, 1)
    total, momentum_out, grid, other_grid = lax.optimization_barrier((total, momentum_out, grid, other_grid))
    decoded = decode(grid, back_cols, back_rows)
    other = decode(other_grid, back_cols, back_rows)
    total = total + along_x(total, 3)
    total, decoded, other = lax.optimization_barrier((total, decoded, other))
    total = total + across(total)
    given = turn(total, "dp", REPLICAS, 1)
    update = rescale(decoded, other, total)
    update = rescale(decoded, other, given, update)
    return (momentum_out[None], update)


def solution(mesh):
    placed = (
        P("dp", None, None, "tensor"),
        P("dp", None, None, "tensor"),
        P(None, None, None, "tensor", None),
    )
    return jax.shard_map(
        on_device,
        mesh=mesh,
        in_specs=placed,
        out_specs=(P("dp", None, None, "tensor"), P(None, None, "tensor")),
        check_vma=False,
    )
```
